256 devices in a mesh: seq: 16 (over y, x), head: 16 (over z, core).
Axes of the slice: x: 4, y: 4, z: 8, core: 2. Of those that a mesh axis runs over, the one named last changes fastest.
Arguments:
- x_in: bfloat16 [2, 4096, 8192], P(None, ('seq', 'head')), may hold values from -6 to 6
- b_in: bfloat16 [2, 4096, 2048], P(None, ('seq', 'head')), may hold values from -6 to 6
- c_in: bfloat16 [2, 4096, 2048], P(None, ('seq', 'head')), may hold values from -0.375 to 0.375
- dt_in: bfloat16 [2, 4096, 128], P(None, ('seq', 'head')), may hold values from -7 to 5
- a_log: float32 [128], P('head'), may hold values from -6 to -2
- skip_gain: float32 [128], P('head'), may hold values from 0.5 to 1.5
- grad_y: bfloat16 [2, 4096, 8192], P(None, 'seq', 'head'), may hold values from -4 to 4
Outputs:
- y_out: bfloat16 [2, 4096, 8192], P(None, 'seq', 'head')
- grad_x: bfloat16 [2, 4096, 8192], P(None, ('seq', 'head'))
- grad_b: bfloat16 [2, 4096, 2048], P(None, ('seq', 'head'))
- grad_c: bfloat16 [2, 4096, 2048], P(None, ('seq', 'head'))
- grad_dt: bfloat16 [2, 4096, 128], P(None, ('seq', 'head'))
The draws below stay inside these ranges and needn't reach their ends.
All inputs are finite; a program needn't handle non-finite values.
Results may differ from the reference program's by a relative error of at most 0.003.
Values may be sent and summed in bfloat16 or wider, within the bound.
A program may use at most 128 MiB of HBM per device.

```python
import math
from functools import partial
import jax
import jax.numpy as jnp
from jax import lax

HEADS = 128
HEAD_DIM = 64
STATE = 256
GROUPS = 8
STRETCH = 256
SEQUENCE_COUNT = 2
SEQUENCE_LENGTH = 4096
N_HEAD = 16


def head_rates(key, exponent):
    decay_speeds = jax.random.uniform(key, (HEADS,), jnp.float32) ** exponent
    lowest = 0.8 / SEQUENCE_LENGTH
    rates = lowest * (0.025 / lowest) ** decay_speeds
    dt_scale = 0.25 * (rates / 0.025) ** 0.6
    return (rates, dt_scale)


def draw_a_log(key, part):
    exponent = 2.5
    rates, dt_scale = head_rates(key, exponent)
    return jnp.log(rates / dt_scale).astype(jnp.float32)


def draw_dt_in(key, part):
    exponent = 2.5
    rates, dt_scale = head_rates(key, exponent)
    key = jax.random.fold_in(key, 11)
    factor_random_key, random_key_split = jax.random.split(key)
    factor = jnp.exp(jax.random.uniform(factor_random_key, (SEQUENCE_COUNT, SEQUENCE_LENGTH, HEADS), jnp.float32, math.log(0.5), math.log(2.0)))
    token_positions = jax.random.randint(random_key_split, (SEQUENCE_COUNT, 4), 0, SEQUENCE_LENGTH)
    marked = jnp.any(jnp.arange(SEQUENCE_LENGTH)[None, :, None] == token_positions[:, None, :], axis=2)
    boost = jnp.where(marked, 8.0, 1.0)
    values = dt_scale[None, None, :] * factor * boost[:, :, None]
    return jnp.log(jnp.expm1(values)).astype(jnp.bfloat16)


def shard_levels(rng, shape, cuts, smallest, largest):
    gain = 1.0
    for axis_at, blocks in cuts:
        draws = jax.random.uniform(jax.random.fold_in(jax.random.fold_in(rng, 6), axis_at), (blocks,), jnp.float32, smallest / len(cuts), largest / len(cuts))
        gain = gain * jnp.repeat(jnp.exp(draws), shape[axis_at] // blocks).reshape((-1,) + (1,) * (len(shape) - 1 - axis_at))
    return gain


def noise(rng, dims, deviation, bound, cuts=(), kind=jnp.bfloat16):
    entries = jax.random.normal(rng, dims, jnp.float32) * deviation
    if len(cuts) > 0:
        entries = shard_levels(rng, dims, cuts, -0.22, 0.18) * entries
    return jnp.clip(entries, min=-bound, max=bound).astype(kind)


def setup_inputs(seed: int = 0) -> dict:
    streams_of = jax.random.split(jax.random.key(seed), 8)
    x_in = noise(streams_of[0], (SEQUENCE_COUNT, SEQUENCE_LENGTH, HEADS * HEAD_DIM), 1.0, 6.0, ((1, 256),))
    b_in = noise(streams_of[1], (SEQUENCE_COUNT, SEQUENCE_LENGTH, GROUPS * STATE), 1.0, 6.0, ((1, 256),))
    c_in = noise(streams_of[2], (SEQUENCE_COUNT, SEQUENCE_LENGTH, GROUPS * STATE), STATE ** -0.5, 0.375, ((1, 256),))
    dt_in = draw_dt_in(jax.random.fold_in(streams_of[7], 71), 0)
    a_log = draw_a_log(jax.random.fold_in(streams_of[7], 71), 0)
    skip_gain = jnp.clip(0.5 + 1.0 * jax.random.uniform(streams_of[5], (HEADS,), jnp.float32) ** shard_levels(streams_of[5], (HEADS,), ((0, 16),), -0.2, 0.2), 0.5, 1.5)
    grad_y = noise(streams_of[6], (SEQUENCE_COUNT, SEQUENCE_LENGTH, HEADS * HEAD_DIM), 0.25, 4.0, ((1, 16), (2, 16)))
    return {"x_in": x_in, "b_in": b_in, "c_in": c_in, "dt_in": dt_in, "a_log": a_log, "skip_gain": skip_gain, "grad_y": grad_y}


highest = lax.Precision.HIGHEST

def carry_state(carried, x_vals, b_vals, dt_vals, cum_vals):
    final_cum = cum_vals[-1]
    weight = jnp.exp(final_cum[None] - cum_vals) * dt_vals
    update = jnp.einsum('tjep,tjn->jepn', x_vals * weight[..., None], b_vals, precision=highest)
    return jnp.exp(final_cum)[..., None, None] * carried + update

def stretched_step_update(carried, x_vals, b_vals, c_vals, dt_vals, cum_vals, skip_rows):
    scores = jnp.einsum('tjn,ujn->jtu', c_vals, b_vals, precision=highest)
    token_positions = jnp.arange(x_vals.shape[0])
    causal = token_positions[:, None] >= token_positions[None, :]
    cum_rows = jnp.moveaxis(cum_vals, 0, 2)
    log_gap = cum_rows[..., :, None] - cum_rows[..., None, :]
    decays = jnp.where(causal, jnp.exp(jnp.where(causal, log_gap, 0.0)), 0.0)
    mixing = scores[:, None] * decays * jnp.moveaxis(dt_vals, 0, 2)[:, :, None, :]
    within = jnp.einsum('jetu,ujep->tjep', mixing, x_vals, precision=highest)
    carried_part = jnp.einsum('tjn,jepn->tjep', c_vals, carried, precision=highest) * jnp.exp(cum_vals)[..., None]
    result = within + carried_part + skip_rows[:, :, None] * x_vals
    return (carry_state(carried, x_vals, b_vals, dt_vals, cum_vals), result)

def scan_step(carried, inputs, decay_rate, skip_rows):
    x_vals, b_vals, c_vals, dt_raw = inputs
    dt_vals = jax.nn.softplus(dt_raw.astype(jnp.float32))
    cum_vals = jnp.cumsum(dt_vals * decay_rate, axis=1)

    def single(state_one, x_one, b_one, c_one, dt_one, cum_one):
        return stretched_step_update(state_one, x_one, b_one, c_one, dt_one, cum_one, skip_rows)
    return jax.vmap(single)(carried, x_vals.astype(jnp.float32), b_vals.astype(jnp.float32), c_vals.astype(jnp.float32), dt_vals, cum_vals)

def reference(x_in, b_in, c_in, dt_in, a_log, skip_gain, grad_y):
    seq_count, length = (x_in.shape[0], x_in.shape[1])
    repeat = N_HEAD // GROUPS
    heads_dev = HEADS // N_HEAD
    stretches = length // STRETCH
    decay_rate = -jnp.exp(a_log).reshape(N_HEAD, heads_dev)
    skip_rows = skip_gain.reshape(N_HEAD, heads_dev)
    stepper = jax.checkpoint(partial(scan_step, decay_rate=decay_rate, skip_rows=skip_rows))

    def spread_groups(array):
        return jnp.repeat(array.reshape(seq_count, length, GROUPS, STATE).astype(jnp.float32), repeat, axis=2)

    def by_stretch(array):
        return jnp.moveaxis(array.reshape((seq_count, stretches, STRETCH) + array.shape[2:]), 1, 0)

    def run_mixer(x_vals, b_vals, c_vals, dt_vals):
        start = jnp.zeros((seq_count, N_HEAD, heads_dev, HEAD_DIM, STATE), jnp.float32)
        final_state, outputs = lax.scan(stepper, start, (by_stretch(x_vals.reshape(seq_count, length, N_HEAD, heads_dev, HEAD_DIM)), by_stretch(b_vals), by_stretch(c_vals), by_stretch(dt_vals.reshape(seq_count, length, N_HEAD, heads_dev))))
        return jnp.moveaxis(outputs, 0, 1).reshape(seq_count, length, HEADS * HEAD_DIM)
    mixed_out, pullback = jax.vjp(run_mixer, x_in, spread_groups(b_in), spread_groups(c_in), dt_in)
    grad_x, slices_b, slices_c, grad_dt = pullback(grad_y.astype(jnp.float32))

    def group_sum(slices):
        rounded = lax.optimization_barrier(slices.astype(jnp.bfloat16))
        summed = rounded.astype(jnp.float32).reshape(seq_count, length, GROUPS, repeat, STATE).sum(axis=3)
        return summed.astype(jnp.bfloat16).reshape(seq_count, length, GROUPS * STATE)
    return (mixed_out.astype(jnp.bfloat16), grad_x, group_sum(slices_b), group_sum(slices_c), grad_dt)
```

```python
from types import SimpleNamespace

import jax
import jax.numpy as jnp
from jax import lax
from jax.experimental import pallas as pl
from jax.experimental.pallas import tpu as pltpu
from jax.sharding import PartitionSpec as P

HEAD_DIM = 64
STATE = 256
STRETCH = 256
LANES = 128
MESH = pl.DeviceIdType.MESH
F32 = jnp.float32
BF16 = jnp.bfloat16
NN = (((1,), (0,)), ((), ()))
NT = (((1,), (1,)), ((), ()))
TN = (((0,), (0,)), ((), ()))


def dot(a, b, dims=NN):
    return lax.dot_general(a, b, dims, preferred_element_type=F32)


def split(value, count):
    parts = []
    for _ in range(count):
        part = value.astype(BF16)
        parts.append(part)
        value = value - part.astype(F32)
    return parts


def dot_split(a, b, dims=NN):
    a_parts = [a] if a.dtype == BF16 else split(a, 2)
    b_parts = [b] if b.dtype == BF16 else split(b, 2)
    total = dot(a_parts[0], b_parts[0], dims)
    for i, left in enumerate(a_parts):
        for j, right in enumerate(b_parts):
            if i + j == 1:
                total = total + dot(left, right, dims)
    return total


def times_exact(value, ones):
    first, second, third = split(value, 3)
    return dot(first, ones) + (dot(second, ones) + dot(third, ones))


def exact_times(ones, value):
    first, second, third = split(value, 3)
    return dot(ones, first) + (dot(ones, second) + dot(ones, third))


def iota(shape, axis):
    return lax.broadcasted_iota(jnp.int32, shape, axis)


def one_hot(condition):
    return jnp.where(condition, 1.0, 0.0).astype(BF16)


def mixer(dims, names, *refs):
    r = SimpleNamespace(**dict(zip(names, refs)))
    ns, nh, seqs, rows, heads = dims
    width = heads * HEAD_DIM
    part = STATE // ns
    chips = nh // 2
    s, h = lax.axis_index("seq"), lax.axis_index("head")
    core = lax.rem(h, 2)
    chip = h // 2
    other = (s, h + 1 - 2 * core)

    def head_peer(k):
        return lax.rem(h + k, nh)

    def seq_peer(k):
        return lax.rem(s + k, ns)

    def remote(src, dst, sem, device):
        pltpu.make_async_remote_copy(
            src, dst, r.send_sem.at[sem], r.recv_sem.at[sem], device_id=device, device_id_type=MESH
        ).start()

    def local(src, dst, sem):
        copy = pltpu.make_async_copy(src, dst, r.local_sem.at[sem])
        copy.start()
        return copy

    def arrived(ref, sem):
        pltpu.make_async_copy(ref, ref, r.recv_sem.at[sem]).wait()

    def left(ref, sem):
        pltpu.make_async_copy(ref, ref, r.send_sem.at[sem]).wait()

    def over(count, body, start=0, step=1):
        def one(i, carry):
            body(start + i * step)
            return carry

        lax.fori_loop(0, count, one, 0)

    def columns(index, size):
        return pl.ds(pl.multiple_of(index * size, size), size)

    DT, C, C2, B, B2, TOT = range(6)
    X, G, D, F, S, GX, GB, GC, GD = (6 + seqs * i for i in range(9))

    barrier = pltpu.get_barrier_semaphore()

    def greet_head(k):
        pl.semaphore_signal(barrier, inc=1, device_id=(s, head_peer(k)), device_id_type=MESH)

    def greet_seq(k):
        pl.semaphore_signal(barrier, inc=1, device_id=(seq_peer(k), h), device_id_type=MESH)

    over(nh - 1, greet_head, 1)
    over(ns - 1, greet_seq, 1)

    own = [
        local(r.dt_in, r.dt_all.at[:, h], 0),
        local(r.c_in.at[:, :, columns(chip, STATE)], r.c_all.at[:, chip, core], 1),
        local(r.b_in.at[:, :, columns(chip, STATE)], r.b_all.at[:, chip, core], 2),
        local(r.x_in.at[:, :, columns(h, width)], r.x_all.at[:, h], 3),
        local(r.gy_in, r.gy, 4),
    ]

    pl.semaphore_wait(barrier, nh - 1 + ns - 1)

    def send_dt(k):
        remote(r.dt_in, r.dt_all.at[:, h], DT, (s, head_peer(k)))

    def send_c(k):
        peer = head_peer(k)
        remote(r.c_in.at[:, :, columns(peer // 2, STATE)], r.c_all.at[:, chip, core], C, (s, peer))

    def send_b(k):
        peer = head_peer(k)
        remote(r.b_in.at[:, :, columns(peer // 2, STATE)], r.b_all.at[:, chip, core], B, (s, peer))

    over(nh - 1, send_dt, 1)
    over(chips - 1, send_c, 2, 2)
    over(chips - 1, send_b, 2, 2)
    for q in range(seqs):

        def send_x(k, q=q):
            peer = head_peer(k)
            remote(r.x_in.at[q, :, columns(peer, width)], r.x_all.at[q, h], X + q, (s, peer))

        over(nh - 1, send_x, 1)

    lane_row = iota((1, LANES), 1)
    rate = jnp.zeros((1, LANES), F32)
    skip_row = jnp.zeros((1, width), F32)
    wide_row = iota((1, width), 1) // HEAD_DIM
    for e in range(heads):
        rate = jnp.where(lane_row == e, r.a_log[e], rate)
        skip_row = jnp.where(wide_row == e, r.skip[e], skip_row)
    rate = jnp.where(lane_row < heads, -jnp.exp(rate), 0.0)
    spread = one_hot(iota((LANES, width), 0) == iota((LANES, width), 1) // HEAD_DIM)
    gather = one_hot(iota((width, LANES), 0) // HEAD_DIM == iota((width, LANES), 1))
    causal = iota((STRETCH, STRETCH), 0) >= iota((STRETCH, STRETCH), 1)
    lower = one_hot(causal)
    upper = one_hot(iota((STRETCH, STRETCH), 0) <= iota((STRETCH, STRETCH), 1))

    own[0].wait()
    arrived(r.dt_all.at[:, 0 : nh - 1], DT)
    all_heads = r.dt_all.shape[3]
    pick_at = (all_heads, LANES)
    pick = one_hot((iota(pick_at, 0) == h * heads + iota(pick_at, 1)) & (iota(pick_at, 1) < heads))
    r.tot_send[...] = jnp.zeros_like(r.tot_send)
    for q in range(seqs):
        raw = dot(r.dt_all[q].reshape(STRETCH, all_heads), pick)
        dt = jnp.maximum(raw, 0.0) + jnp.log1p(jnp.exp(-jnp.abs(raw)))
        cum = exact_times(lower, dt * rate)
        last = cum[STRETCH - 1 :, :]
        r.raw[q] = raw
        r.dt[q] = dt
        r.tot_send[pl.ds(q, 1), :] = last
        r.w_wide[q] = times_exact(jnp.exp(last - cum) * dt, spread)
        r.e_wide[q] = times_exact(jnp.exp(cum), spread)
        r.u_row[q] = jnp.transpose(cum - jnp.log(dt))[:heads, :]
        for e in range(heads):
            r.cum_col[q, e] = jnp.broadcast_to(cum[:, e : e + 1], (STRETCH, LANES))

    def send_tot(k):
        remote(r.tot_send, r.tot_all.at[s], TOT, (seq_peer(k), h))

    over(ns - 1, send_tot, 1)
    r.tot_all[s] = r.tot_send[...]

    own[4].wait()
    own[1].wait()
    arrived(r.c_all.at[:, 0 : chips - 1, 0], C)
    remote(r.c_all.at[:, :, core], r.c_all.at[:, :, core], C2, other)
    for q in range(seqs):
        first, second = split(r.gy[q].astype(F32) * r.e_wide[q], 2)
        r.gys_hi[q] = first
        r.gys_lo[q] = second
        r.gy_t[q] = jnp.transpose(r.gy[q])
    arrived(r.c_all.at[:, :, 0], C2)

    def c_of(q):
        return r.c_all[q].reshape(STRETCH, STATE)

    def b_of(q):
        return r.b_all[q].reshape(STRETCH, STATE)

    def x_of(q):
        return r.x_all[q].reshape(STRETCH, width)

    def send_parts(q, source, target, sem):
        def one(k):
            peer = seq_peer(k)
            remote(source.at[q, columns(peer, part), :], target.at[q, s], sem + q, (peer, h))

        over(ns - 1, one, 1)
        target[q, s] = source[q, columns(s, part), :]

    for q in range(seqs):
        r.g_out[q] = dot(c_of(q), r.gys_hi[q], TN) + dot(c_of(q), r.gys_lo[q], TN)
        send_parts(q, r.g_out, r.g_in, G)

    own[2].wait()
    arrived(r.b_all.at[:, 0 : chips - 1, 0], B)
    remote(r.b_all.at[:, :, core], r.b_all.at[:, :, core], B2, other)
    arrived(r.b_all.at[:, :, 0], B2)

    def decays(q):
        r.scores[q] = dot(c_of(q), b_of(q), NT)

        def one(e):
            column = r.cum_col[q, e]
            gap = jnp.concatenate([column, column], axis=1) - r.u_row[q, pl.ds(e, 1), :]
            decay = jnp.where(causal, jnp.exp(gap), 0.0)
            r.decay[q, e] = decay
            first, second = split(r.scores[q] * decay, 2)
            r.mix_hi[q, e] = first
            r.mix_lo[q, e] = second
            rows_e = columns(e, HEAD_DIM)
            grad = r.gy_t[q, rows_e, :]
            r.z_t[q, rows_e, :] = dot(grad, first) + dot(grad, second)

        over(heads, one)

    def send_state(q):
        arrived(r.x_all.at[q, 0 : nh - 1], X + q)
        first, second = split(x_of(q).astype(F32) * r.w_wide[q], 2)
        r.xs_hi[q] = first
        r.xs_lo[q] = second
        r.f_out[q] = dot(b_of(q), first, TN) + dot(b_of(q), second, TN)
        send_parts(q, r.f_out, r.f_in, F)

    def within(q):
        r.d_scores[q] = jnp.zeros((STRETCH, STRETCH), F32)
        low = iota((STRETCH, LANES), 1) < HEAD_DIM

        def one(i):
            cols = columns(i, LANES)
            x_pair = r.x_all[q, :, :, cols].reshape(STRETCH, LANES)
            grad = r.gy[q, :, cols].astype(F32)
            results = []
            total = r.d_scores[q]
            for k in range(2):
                e = 2 * i + k
                results.append(dot(r.mix_hi[q, e], x_pair) + dot(r.mix_lo[q, e], x_pair))
                masked = jnp.where(low if k == 0 else ~low, grad, 0.0).astype(BF16)
                total = total + dot(masked, x_pair, NT) * r.decay[q, e]
            r.d_scores[q] = total
            r.y_in[q, :, cols] = jnp.where(low, results[0], results[1])

        over(heads // 2, one)

    def scan(q, source, result, target, sem, sem_in, reverse):
        arrived(source.at[q, 0 : ns - 1], sem_in + q)

        def one(i, state):
            block = ns - 1 - i if reverse else i
            result[q, block] = state
            return r.factor[pl.ds(block * 8 + q, 1), :] * state + source[q, block]

        lax.fori_loop(0, ns, one, jnp.zeros((part, width), F32))

        def back(k):
            peer = seq_peer(k)
            remote(result.at[q, peer], target.at[q, columns(s, part), :], sem + q, (peer, h))

        over(ns - 1, back, 1)
        target[q, columns(s, part), :] = result[q, s]

    def states_here(q, target, sem):
        arrived(target.at[q, 0 : (ns - 1) * part, :], sem + q)

    def send_rows(q, source, target_of, sem):
        def one(k):
            peer = head_peer(k)
            remote(source.at[q, columns(peer, rows), :], target_of(q), sem + q, (s, peer))

        over(nh - 1, one, 1)

    def gx_slot(q):
        return r.gx_out.at[q, :, columns(h, width)]

    own_gx = []

    def grad_x(q):
        states_here(q, r.d_all, D)
        r.xc[q] = r.w_wide[q] * dot_split(b_of(q), r.d_all[q])
        r.xp[q] = jnp.transpose(r.z_t[q]) + r.xc[q]
        r.gx[q] = (skip_row * r.gy[q].astype(F32) + r.xp[q]).astype(BF16)
        send_rows(q, r.gx, gx_slot, GX)
        own_gx.append(local(r.gx.at[q, columns(h, rows), :], gx_slot(q), 5 + q))

    def grad_b(q):
        first, second = split(jnp.transpose(r.d_scores[q]), 2)
        value = dot(first, c_of(q)) + dot(second, c_of(q))
        d_hi, d_lo = split(r.d_all[q], 2)
        value = value + dot(r.xs_hi[q], d_hi, NT)
        value = value + (dot(r.xs_hi[q], d_lo, NT) + dot(r.xs_lo[q], d_hi, NT))
        r.gb[q] = value.astype(BF16)
        send_rows(q, r.gb, lambda q: r.gb_all.at[q, h], GB)
        r.gb_all[q, h] = r.gb[q, columns(h, rows), :]

    own_y = []

    def finish(q):
        states_here(q, r.s_all, S)
        s_hi, s_lo = split(r.s_all[q], 2)
        first, second = split(r.d_scores[q], 2)
        value = dot(first, b_of(q)) + dot(second, b_of(q))
        value = value + dot(r.gys_hi[q], s_hi, NT)
        value = value + (dot(r.gys_hi[q], s_lo, NT) + dot(r.gys_lo[q], s_hi, NT))
        r.gc[q] = value.astype(BF16)
        send_rows(q, r.gc, lambda q: r.gc_all.at[q, h], GC)
        r.gc_all[q, h] = r.gc[q, columns(h, rows), :]

        y = r.y_in[q] + r.e_wide[q] * (dot(c_of(q), s_hi) + dot(c_of(q), s_lo))
        x = x_of(q).astype(F32)
        r.y[q] = (y + skip_row * x).astype(BF16)
        own_y.append(local(r.y.at[q], r.y_out.at[q], 5 + seqs + q))

        dt = r.dt[q]
        v = times_exact(x * r.xp[q], gather)
        d_cum = times_exact(r.gy[q].astype(F32) * y, gather) - v
        at_last = jnp.sum(x * r.xc[q], axis=0, keepdims=True) + r.e_wide[q, STRETCH - 1 :, :] * jnp.sum(
            r.s_all[q] * r.d_all[q], axis=0, keepdims=True
        )
        at_last = times_exact(jnp.broadcast_to(at_last, (8, width)), gather)[:1]
        d_sum = exact_times(upper, d_cum) + at_last
        grad = (v / dt + rate * d_sum) * jax.nn.sigmoid(r.raw[q])
        r.gd[q] = grad.astype(BF16)
        send_rows(q, r.gd, lambda q: r.gd_all.at[q, h], GD)
        r.gd_all[q, h] = r.gd[q, columns(h, rows), :]

    for q in range(seqs):
        decays(q)
    own[3].wait()
    send_state(0)
    arrived(r.tot_all.at[0 : ns - 1], TOT)
    r.factor[...] = jnp.exp(times_exact(r.tot_all[...].reshape(ns * 8, LANES), spread))
    scan(0, r.g_in, r.g_res, r.d_all, D, G, True)
    within(0)
    send_state(1)
    scan(1, r.g_in, r.g_res, r.d_all, D, G, True)
    grad_x(0)
    scan(0, r.f_in, r.f_res, r.s_all, S, F, False)
    within(1)
    grad_b(0)
    grad_x(1)
    scan(1, r.f_in, r.f_res, r.s_all, S, F, False)
    grad_b(1)
    finish(0)
    finish(1)

    for q in range(seqs):
        arrived(r.gb_all.at[q, 0 : nh - 1], GB + q)
        for g in range(chips):
            both = r.gb_all[q, 2 * g].astype(F32) + r.gb_all[q, 2 * g + 1].astype(F32)
            r.gb_out[q, :, g * STATE : (g + 1) * STATE] = both.astype(BF16)
    for q in range(seqs):
        arrived(r.gc_all.at[q, 0 : nh - 1], GC + q)
        for g in range(chips):
            both = r.gc_all[q, 2 * g].astype(F32) + r.gc_all[q, 2 * g + 1].astype(F32)
            r.gc_out[q, :, g * STATE : (g + 1) * STATE] = both.astype(BF16)
    place_at = (LANES, all_heads)
    for q in range(seqs):
        arrived(r.gd_all.at[q, 0 : nh - 1], GD + q)
        total = jnp.zeros((rows, all_heads), F32)
        for p in range(nh):
            place = one_hot((iota(place_at, 1) == p * heads + iota(place_at, 0)) & (iota(place_at, 0) < heads))
            total = total + dot(r.gd_all[q, p], place)
        r.gdt_out[q] = total.astype(BF16)
    for q in range(seqs):
        arrived(r.gx_out.at[q, :, 0 : (nh - 1) * width], GX + q)

    left(r.dt_all.at[:, 0 : nh - 1], DT)
    left(r.c_all.at[:, 0 : chips - 1, 0], C)
    left(r.c_all.at[:, :, 0], C2)
    left(r.b_all.at[:, 0 : chips - 1, 0], B)
    left(r.b_all.at[:, :, 0], B2)
    left(r.tot_all.at[0 : ns - 1], TOT)
    for q in range(seqs):
        left(r.x_all.at[q, 0 : nh - 1], X + q)
        left(r.g_in.at[q, 0 : ns - 1], G + q)
        left(r.g_res.at[q, 0 : ns - 1], D + q)
        left(r.f_in.at[q, 0 : ns - 1], F + q)
        left(r.f_res.at[q, 0 : ns - 1], S + q)
        left(r.gx.at[q, 0 : (nh - 1) * rows, :], GX + q)
        left(r.gb_all.at[q, 0 : nh - 1], GB + q)
        left(r.gc_all.at[q, 0 : nh - 1], GC + q)
        left(r.gd_all.at[q, 0 : nh - 1], GD + q)
    for copy in own_gx + own_y:
        copy.wait()


def on_device(x_in, b_in, c_in, dt_in, a_log, skip_gain, grad_y):
    ns, nh = lax.axis_size("seq"), lax.axis_size("head")
    seqs, rows, all_heads = dt_in.shape
    heads = a_log.shape[0]
    width = heads * HEAD_DIM
    part = STATE // ns
    chips = nh // 2
    scratch = {
        "dt_all": ((seqs, nh, rows, all_heads), BF16),
        "c_all": ((seqs, chips, 2, rows, STATE), BF16),
        "b_all": ((seqs, chips, 2, rows, STATE), BF16),
        "x_all": ((seqs, nh, rows, width), BF16),
        "gy": ((seqs, STRETCH, width), BF16),
        "gy_t": ((seqs, width, STRETCH), BF16),
        "raw": ((seqs, STRETCH, LANES), F32),
        "dt": ((seqs, STRETCH, LANES), F32),
        "tot_send": ((8, LANES), F32),
        "tot_all": ((ns, 8, LANES), F32),
        "factor": ((ns * 8, width), F32),
        "w_wide": ((seqs, STRETCH, width), F32),
        "e_wide": ((seqs, STRETCH, width), F32),
        "u_row": ((seqs, heads, STRETCH), F32),
        "cum_col": ((seqs, heads, STRETCH, LANES), F32),
        "gys_hi": ((seqs, STRETCH, width), BF16),
        "gys_lo": ((seqs, STRETCH, width), BF16),
        "xs_hi": ((seqs, STRETCH, width), BF16),
        "xs_lo": ((seqs, STRETCH, width), BF16),
        "scores": ((seqs, STRETCH, STRETCH), F32),
        "d_scores": ((seqs, STRETCH, STRETCH), F32),
        "decay": ((seqs, heads, STRETCH, STRETCH), F32),
        "mix_hi": ((seqs, heads, STRETCH, STRETCH), BF16),
        "mix_lo": ((seqs, heads, STRETCH, STRETCH), BF16),
        "z_t": ((seqs, width, STRETCH), F32),
        "xc": ((seqs, STRETCH, width), F32),
        "xp": ((seqs, STRETCH, width), F32),
        "y_in": ((seqs, STRETCH, width), F32),
        "y": ((seqs, STRETCH, width), BF16),
        "gx": ((seqs, STRETCH, width), BF16),
        "gb": ((seqs, STRETCH, STATE), BF16),
        "gc": ((seqs, STRETCH, STATE), BF16),
        "gd": ((seqs, STRETCH, LANES), BF16),
        "gb_all": ((seqs, nh, rows, STATE), BF16),
        "gc_all": ((seqs, nh, rows, STATE), BF16),
        "gd_all": ((seqs, nh, rows, LANES), BF16),
    }
    for name in ("g", "f"):
        scratch[name + "_out"] = ((seqs, STATE, width), F32)
        scratch[name + "_in"] = ((seqs, ns, part, width), F32)
        scratch[name + "_res"] = ((seqs, ns, part, width), F32)
    for name in ("d_all", "s_all"):
        scratch[name] = ((seqs, STATE, width), F32)
    sems = 6 + 9 * seqs
    names = (
        ["a_log", "skip", "x_in", "b_in", "c_in", "dt_in", "gy_in"]
        + ["y_out", "gx_out", "gb_out", "gc_out", "gdt_out"]
        + list(scratch)
        + ["send_sem", "recv_sem", "local_sem"]
    )
    dims = (ns, nh, seqs, rows, heads)

    def body(*refs):
        mixer(dims, names, *refs)

    anywhere = pl.BlockSpec(memory_space=pl.ANY)
    small = pl.BlockSpec(memory_space=pltpu.SMEM)
    vmem = pl.BlockSpec(memory_space=pltpu.VMEM)

    def like(array):
        return jax.ShapeDtypeStruct(array.shape, BF16)

    return pl.pallas_call(
        body,
        out_shape=(like(grad_y), like(x_in), like(b_in), like(c_in), like(dt_in)),
        in_specs=[small, small] + [anywhere] * 5,
        out_specs=(anywhere, anywhere, vmem, vmem, vmem),
        scratch_shapes=[pltpu.VMEM(shape, dtype) for shape, dtype in scratch.values()]
        + [
            pltpu.SemaphoreType.DMA((sems,)),
            pltpu.SemaphoreType.DMA((sems,)),
            pltpu.SemaphoreType.DMA((5 + 2 * seqs,)),
        ],
        compiler_params=pltpu.CompilerParams(
            collective_id=0, has_side_effects=True, vmem_limit_bytes=56 * 1024 * 1024
        ),
        name="mixer",
    )(a_log, skip_gain, x_in, b_in, c_in, dt_in, grad_y)


def solution(mesh):
    spread = P(None, ("seq", "head"), None)
    return jax.shard_map(
        on_device,
        mesh=mesh,
        in_specs=(spread, spread, spread, spread, P("head"), P("head"), P(None, "seq", "head")),
        out_specs=(P(None, "seq", "head"), spread, spread, spread, spread),
        check_vma=False,
    )
```

```python
from types import SimpleNamespace

import jax
import jax.numpy as jnp
from jax import lax
from jax.experimental import pallas as pl
from jax.experimental.pallas import tpu as pltpu
from jax.sharding import PartitionSpec as P

HEAD_DIM = 64
STATE = 256
STRETCH = 256
LANES = 128
MESH = pl.DeviceIdType.MESH
F32 = jnp.float32
BF16 = jnp.bfloat16
NN = (((1,), (0,)), ((), ()))
NT = (((1,), (1,)), ((), ()))
TN = (((0,), (0,)), ((), ()))
LN2 = 0.6931471805599453
TINY = 1e-30
CODE_SPAN = 252.0
X_B = 6.0 * 6.0 * 1.001
GY_C = 4.0 * 0.375 * 1.001


def dot(a, b, dims=NN):
    return lax.dot_general(a, b, dims, preferred_element_type=F32)


def split(value, count):
    parts = []
    for _ in range(count):
        part = value.astype(BF16)
        parts.append(part)
        value = value - part.astype(F32)
    return parts


def dot_split(a, b, dims=NN):
    a_parts = [a] if a.dtype == BF16 else split(a, 2)
    b_parts = [b] if b.dtype == BF16 else split(b, 2)
    total = dot(a_parts[0], b_parts[0], dims)
    for i, left in enumerate(a_parts):
        for j, right in enumerate(b_parts):
            if i + j == 1:
                total = total + dot(left, right, dims)
    return total


def times_exact(value, ones):
    first, second, third = split(value, 3)
    return dot(first, ones) + (dot(second, ones) + dot(third, ones))


def exact_times(ones, value):
    first, second, third = split(value, 3)
    return dot(ones, first) + (dot(ones, second) + dot(ones, third))


def encode(value, bound):
    share = jnp.maximum(jnp.abs(value) / jnp.maximum(bound, TINY), TINY)
    level = jnp.exp2(jnp.log(share) * (0.125 / LN2))
    code = jnp.exp2(level * CODE_SPAN - 0.5 * CODE_SPAN)
    return jnp.where(value < 0.0, -code, code).astype(BF16)


def decode(code, bound):
    code = code.astype(F32)
    level = jnp.maximum(jnp.log(jnp.abs(code)) * (1.0 / (LN2 * CODE_SPAN)) + 0.5, 0.0)
    square = level * level
    square = square * square
    size = square * square * bound
    return jnp.where(code < 0.0, -size, size)


def iota(shape, axis):
    return lax.broadcasted_iota(jnp.int32, shape, axis)


def one_hot(condition):
    return jnp.where(condition, 1.0, 0.0).astype(BF16)


def mixer(dims, names, *refs):
    r = SimpleNamespace(**dict(zip(names, refs)))
    ns, nh, seqs, rows, heads = dims
    width = heads * HEAD_DIM
    part = STATE // ns
    chips = nh // 2
    s, h = lax.axis_index("seq"), lax.axis_index("head")
    core = lax.rem(h, 2)
    chip = h // 2
    other = (s, h + 1 - 2 * core)

    def head_peer(k):
        return lax.rem(h + k, nh)

    def seq_peer(k):
        return lax.rem(s + k, ns)

    def remote(src, dst, sem, device):
        pltpu.make_async_remote_copy(
            src, dst, r.send_sem.at[sem], r.recv_sem.at[sem], device_id=device, device_id_type=MESH
        ).start()

    def local(src, dst, sem):
        copy = pltpu.make_async_copy(src, dst, r.local_sem.at[sem])
        copy.start()
        return copy

    def arrived(ref, sem):
        pltpu.make_async_copy(ref, ref, r.recv_sem.at[sem]).wait()

    def left(ref, sem):
        pltpu.make_async_copy(ref, ref, r.send_sem.at[sem]).wait()

    def over(count, body, start=0, step=1):
        def one(i, carry):
            body(start + i * step)
            return carry

        lax.fori_loop(0, count, one, 0)

    def columns(index, size):
        return pl.ds(pl.multiple_of(index * size, size), size)

    DT, C, C2, B, B2, TOT, GD = range(7)
    X, G, D, F, S, GX, GB, GC, GB2, GC2 = (7 + seqs * i for i in range(10))

    barrier = pltpu.get_barrier_semaphore()

    def greet_head(k):
        pl.semaphore_signal(barrier, inc=1, device_id=(s, head_peer(k)), device_id_type=MESH)

    def greet_seq(k):
        pl.semaphore_signal(barrier, inc=1, device_id=(seq_peer(k), h), device_id_type=MESH)

    over(nh - 1, greet_head, 1)
    over(ns - 1, greet_seq, 1)

    own = [
        local(r.c_in.at[:, :, columns(chip, STATE)], r.c_all.at[:, chip, core], 0),
        local(r.b_in.at[:, :, columns(chip, STATE)], r.b_all.at[:, chip, core], 1),
        local(r.x_in.at[:, :, columns(h, width)], r.x_all.at[:, h], 2),
        local(r.gy_in, r.gy, 3),
    ]

    all_heads = r.dt_in.shape[2]
    pack_lane = iota((rows, all_heads), 1)
    raw_dt = [r.dt_in[q].astype(F32) for q in range(seqs)]
    for p in range(nh):
        packed = jnp.zeros((rows, all_heads), F32)
        for q in range(seqs):
            moved = pltpu.roll(raw_dt[q], (q - p) * heads % all_heads, 1)
            packed = jnp.where(pack_lane // heads == q, moved, packed)
        r.dt_pack[p] = packed.astype(BF16)
    r.dt_all[h] = r.dt_pack[h]
    own[3].wait()
    for q in range(seqs):
        r.gy_t[q] = jnp.transpose(r.gy[q])

    pl.semaphore_wait(barrier, nh - 1 + ns - 1)

    def send_dt(k):
        peer = head_peer(k)
        remote(r.dt_pack.at[peer], r.dt_all.at[h], DT, (s, peer))

    def send_c(k):
        peer = head_peer(k)
        remote(r.c_in.at[:, :, columns(peer // 2, STATE)], r.c_all.at[:, chip, core], C, (s, peer))

    def send_b(k):
        peer = head_peer(k)
        remote(r.b_in.at[:, :, columns(peer // 2, STATE)], r.b_all.at[:, chip, core], B, (s, peer))

    over(nh - 1, send_dt, 1)
    over(chips - 1, send_c, 2, 2)
    over(chips - 1, send_b, 2, 2)
    for q in range(seqs):

        def send_x(k, q=q):
            peer = head_peer(k)
            remote(r.x_in.at[q, :, columns(peer, width)], r.x_all.at[q, h], X + q, (s, peer))

        over(nh - 1, send_x, 1)

    lane_row = iota((1, LANES), 1)
    rate = jnp.zeros((1, LANES), F32)
    skip_row = jnp.zeros((1, width), F32)
    wide_row = iota((1, width), 1) // HEAD_DIM
    for e in range(heads):
        rate = jnp.where(lane_row == e, r.a_log[e], rate)
        skip_row = jnp.where(wide_row == e, r.skip[e], skip_row)
    rate = jnp.where(lane_row < heads, -jnp.exp(rate), 0.0)
    spread = one_hot(iota((LANES, width), 0) == iota((LANES, width), 1) // HEAD_DIM)
    gather = one_hot(iota((width, LANES), 0) // HEAD_DIM == iota((width, LANES), 1))
    causal = iota((STRETCH, STRETCH), 0) >= iota((STRETCH, STRETCH), 1)
    lower = one_hot(causal)
    upper = one_hot(iota((STRETCH, STRETCH), 0) <= iota((STRETCH, STRETCH), 1))

    arrived(r.dt_all.at[0 : nh - 1], DT)
    raw_all = r.dt_all[...].reshape(STRETCH, all_heads).astype(F32)
    r.tot_send[...] = jnp.zeros_like(r.tot_send)
    for q in range(seqs):
        raw = raw_all if q == 0 else pltpu.roll(raw_all, all_heads - q * heads, 1)
        dt = jnp.maximum(raw, 0.0) + jnp.log1p(jnp.exp(-jnp.abs(raw)))
        cum = exact_times(lower, dt * rate)
        last = cum[STRETCH - 1 :, :]
        r.raw[q] = raw
        r.dt[q] = dt
        weight = jnp.exp(last - cum) * dt
        growth = jnp.exp(cum)
        r.tot_send[pl.ds(q, 1), :] = last
        r.tot_send[pl.ds(seqs + q, 1), :] = X_B * jnp.sum(weight, axis=0, keepdims=True)
        r.tot_send[pl.ds(2 * seqs + q, 1), :] = GY_C * jnp.sum(growth, axis=0, keepdims=True)
        r.w_wide[q] = times_exact(weight, spread)
        r.e_wide[q] = times_exact(growth, spread)
        r.u_row[q] = jnp.transpose(cum - jnp.log(dt))[:heads, :]
        for e in range(heads):
            r.cum_col[q, e] = jnp.broadcast_to(cum[:, e : e + 1], (STRETCH, LANES))

    def send_tot(k):
        remote(r.tot_send, r.tot_all.at[s], TOT, (seq_peer(k), h))

    over(ns - 1, send_tot, 1)
    r.tot_all[s] = r.tot_send[...]
    r.own_wide[...] = times_exact(r.tot_send[...], spread)

    def own_bound(row):
        return r.own_wide[pl.ds(row, 1), :]

    own[0].wait()
    arrived(r.c_all.at[:, 0 : chips - 1, 0], C)
    remote(r.c_all.at[:, :, core], r.c_all.at[:, :, core], C2, other)
    for q in range(seqs):
        first, second = split(r.gy[q].astype(F32) * r.e_wide[q], 2)
        r.gys_hi[q] = first
        r.gys_lo[q] = second
    own[1].wait()
    arrived(r.b_all.at[:, 0 : chips - 1, 0], B)
    remote(r.b_all.at[:, :, core], r.b_all.at[:, :, core], B2, other)
    arrived(r.c_all.at[:, :, 0], C2)

    def c_of(q):
        return r.c_all[q].reshape(STRETCH, STATE)

    def b_of(q):
        return r.b_all[q].reshape(STRETCH, STATE)

    def x_of(q):
        return r.x_all[q].reshape(STRETCH, width)

    def send_parts(q, source, target, sem):
        def one(k):
            peer = seq_peer(k)
            remote(source.at[q, columns(peer, part), :], target.at[q, s], sem + q, (peer, h))

        over(ns - 1, one, 1)
        target[q, s] = source[q, columns(s, part), :]

    for q in range(seqs):
        state = dot(c_of(q), r.gys_hi[q], TN) + dot(c_of(q), r.gys_lo[q], TN)
        r.g_out[q] = encode(state, own_bound(2 * seqs + q))
        send_parts(q, r.g_out, r.g_in, G)

    arrived(r.b_all.at[:, :, 0], B2)

    def decays(q):
        r.scores[q] = dot(c_of(q), b_of(q), NT)

        def one(e):
            column = r.cum_col[q, e]
            gap = jnp.concatenate([column, column], axis=1) - r.u_row[q, pl.ds(e, 1), :]
            decay = jnp.where(causal, jnp.exp(gap), 0.0)
            r.decay[q, e] = decay
            first, second = split(r.scores[q] * decay, 2)
            r.mix_hi[q, e] = first
            r.mix_lo[q, e] = second
            rows_e = columns(e, HEAD_DIM)
            grad = r.gy_t[q, rows_e, :]
            r.z_t[q, rows_e, :] = dot(grad, first) + dot(grad, second)

        over(heads, one)

    def send_state(q):
        arrived(r.x_all.at[q, 0 : nh - 1], X + q)
        first, second = split(x_of(q).astype(F32) * r.w_wide[q], 2)
        r.xs_hi[q] = first
        r.xs_lo[q] = second
        state = dot(b_of(q), first, TN) + dot(b_of(q), second, TN)
        r.f_out[q] = encode(state, own_bound(seqs + q))
        send_parts(q, r.f_out, r.f_in, F)

    def within(q):
        r.d_scores[q] = jnp.zeros((STRETCH, STRETCH), F32)
        low = iota((STRETCH, LANES), 1) < HEAD_DIM

        def one(i):
            cols = columns(i, LANES)
            x_pair = r.x_all[q, :, :, cols].reshape(STRETCH, LANES)
            grad = r.gy[q, :, cols].astype(F32)
            results = []
            total = r.d_scores[q]
            for k in range(2):
                e = 2 * i + k
                results.append(dot(r.mix_hi[q, e], x_pair) + dot(r.mix_lo[q, e], x_pair))
                masked = jnp.where(low if k == 0 else ~low, grad, 0.0).astype(BF16)
                total = total + dot(masked, x_pair, NT) * r.decay[q, e]
            r.d_scores[q] = total
            r.y_in[q, :, cols] = jnp.where(low, results[0], results[1])

        over(heads // 2, one)

    def scan(q, source, result, bounds, target, sem, sem_in, bound_row, reverse):
        arrived(source.at[q, 0 : ns - 1], sem_in + q)

        def wide(block, row):
            return r.wide[pl.ds(block * 8 + row, 1), :]

        def one(i, carry):
            block = ns - 1 - i if reverse else i
            state, bound = carry
            bounds[q, block] = bound
            result[q, block] = encode(state, bound)
            factor = jnp.exp(wide(block, q))
            block_bound = wide(block, bound_row + q)
            return (factor * state + decode(source[q, block], block_bound), factor * bound + block_bound)

        lax.fori_loop(0, ns, one, (jnp.zeros((part, width), F32), jnp.zeros((1, width), F32)), unroll=4)

        def back(k):
            peer = seq_peer(k)
            remote(result.at[q, peer], target.at[q, columns(s, part), :], sem + q, (peer, h))

        over(ns - 1, back, 1)
        target[q, columns(s, part), :] = result[q, s]

    def scan_back(q):
        scan(q, r.g_in, r.g_res, r.d_bound, r.d_code, D, G, 2 * seqs, True)

    def scan_on(q):
        scan(q, r.f_in, r.f_res, r.s_bound, r.s_code, S, F, seqs, False)

    def states_here(q, codes, bounds, target, sem):
        arrived(codes.at[q, 0 : (ns - 1) * part, :], sem + q)
        target[q] = decode(codes[q], bounds[q, s])

    def send_rows(q, source, target_of, sem):
        def one(k):
            peer = head_peer(k)
            remote(source.at[q, columns(peer, rows), :], target_of(q), sem + q, (s, peer))

        over(nh - 1, one, 1)

    def gx_slot(q):
        return r.gx_out.at[q, :, columns(h, width)]

    own_gx = []

    def grad_x(q):
        states_here(q, r.d_code, r.d_bound, r.d_all, D)
        r.xc[q] = r.w_wide[q] * dot_split(b_of(q), r.d_all[q])
        r.xp[q] = jnp.transpose(r.z_t[q]) + r.xc[q]
        r.gx[q] = (skip_row * r.gy[q].astype(F32) + r.xp[q]).astype(BF16)
        send_rows(q, r.gx, gx_slot, GX)
        own_gx.append(local(r.gx.at[q, columns(h, rows), :], gx_slot(q), 4 + q))

    def hand_over(q, value, slices, sem):
        slices[q] = value.astype(BF16).reshape(chips, 2, rows, STATE)
        remote(slices.at[q, :, 1 - core], slices.at[seqs + q, :, 0], sem + q, other)

    own_group = []

    def join(q, slices, sums, out, sem_in, sem, number):
        arrived(slices.at[seqs + q, :, 0], sem_in + q)
        sums[q] = (slices[q, :, core].astype(F32) + slices[seqs + q, :, 0].astype(F32)).astype(BF16)

        def slot():
            return out.at[q, :, columns(chip, STATE)]

        def one(k):
            peer = head_peer(k)
            remote(sums.at[q, peer // 2], slot(), sem + q, (s, peer))

        over(chips - 1, one, 2, 2)
        own_group.append(local(sums.at[q, chip], slot(), number))

    def grad_b(q):
        first, second = split(jnp.transpose(r.d_scores[q]), 2)
        value = dot(first, c_of(q)) + dot(second, c_of(q))
        d_hi, d_lo = split(r.d_all[q], 2)
        value = value + dot(r.xs_hi[q], d_hi, NT)
        value = value + (dot(r.xs_hi[q], d_lo, NT) + dot(r.xs_lo[q], d_hi, NT))
        hand_over(q, value, r.gb, GB2)

    def join_b(q):
        join(q, r.gb, r.gb_sum, r.gb_out, GB2, GB, 4 + seqs + q)

    def join_c(q):
        join(q, r.gc, r.gc_sum, r.gc_out, GC2, GC, 4 + 2 * seqs + q)

    def grad_c(q):
        states_here(q, r.s_code, r.s_bound, r.s_all, S)
        s_hi, s_lo = split(r.s_all[q], 2)
        first, second = split(r.d_scores[q], 2)
        value = dot(first, b_of(q)) + dot(second, b_of(q))
        value = value + dot(r.gys_hi[q], s_hi, NT)
        value = value + (dot(r.gys_hi[q], s_lo, NT) + dot(r.gys_lo[q], s_hi, NT))
        hand_over(q, value, r.gc, GC2)

    def outputs(q):
        y = r.y_in[q] + r.e_wide[q] * dot_split(c_of(q), r.s_all[q])
        x = x_of(q).astype(F32)
        r.y_out[q] = (y + skip_row * x).astype(BF16)

        dt = r.dt[q]
        v = times_exact(x * r.xp[q], gather)
        d_cum = times_exact(r.gy[q].astype(F32) * y, gather) - v
        at_last = jnp.sum(x * r.xc[q], axis=0, keepdims=True) + r.e_wide[q, STRETCH - 1 :, :] * jnp.sum(
            r.s_all[q] * r.d_all[q], axis=0, keepdims=True
        )
        at_last = times_exact(jnp.broadcast_to(at_last, (8, width)), gather)[:1]
        d_sum = exact_times(upper, d_cum) + at_last
        r.gd_wide[q] = (v / dt + rate * d_sum) * jax.nn.sigmoid(r.raw[q])

    def send_steps():
        lane = iota((STRETCH, LANES), 1)
        packed = r.gd_wide[0]
        for q in range(1, seqs):
            packed = jnp.where(lane // heads == q, pltpu.roll(r.gd_wide[q], q * heads, 1), packed)
        r.gd[...] = packed.astype(BF16)

        def one(k):
            peer = head_peer(k)
            remote(r.gd.at[columns(peer, rows), :], r.gd_all.at[h], GD, (s, peer))

        over(nh - 1, one, 1)
        r.gd_all[h] = r.gd[columns(h, rows), :]

    decays(0)
    arrived(r.tot_all.at[0 : ns - 1], TOT)
    r.wide[...] = times_exact(r.tot_all[...].reshape(ns * 8, LANES), spread)
    decays(1)
    scan_back(0)
    scan_back(1)
    own[2].wait()
    send_state(0)
    within(0)
    send_state(1)
    grad_x(0)
    grad_x(1)
    scan_on(0)
    within(1)
    grad_b(0)
    scan_on(1)
    grad_b(1)
    join_b(0)
    join_b(1)
    grad_c(0)
    outputs(0)
    join_c(0)
    grad_c(1)
    outputs(1)
    send_steps()
    join_c(1)

    arrived(r.gd_all.at[0 : nh - 1], GD)
    for q in range(seqs):
        total = jnp.zeros((rows, all_heads), F32)
        for p in range(nh):
            moved = pltpu.roll(r.gd_all[p].astype(F32), (p - q) * heads % LANES, 1)[:, :all_heads]
            total = jnp.where(pack_lane // heads == p, moved, total)
        r.gdt_out[q] = total.astype(BF16)
    for q in range(seqs):
        arrived(r.gx_out.at[q, :, 0 : (nh - 1) * width], GX + q)
        arrived(r.gb_out.at[q, :, 0 : (chips - 1) * STATE], GB + q)
        arrived(r.gc_out.at[q, :, 0 : (chips - 1) * STATE], GC + q)

    left(r.dt_all.at[0 : nh - 1], DT)
    left(r.gd_all.at[0 : nh - 1], GD)
    left(r.c_all.at[:, 0 : chips - 1, 0], C)
    left(r.c_all.at[:, :, 0], C2)
    left(r.b_all.at[:, 0 : chips - 1, 0], B)
    left(r.b_all.at[:, :, 0], B2)
    left(r.tot_all.at[0 : ns - 1], TOT)
    for q in range(seqs):
        left(r.x_all.at[q, 0 : nh - 1], X + q)
        left(r.g_in.at[q, 0 : ns - 1], G + q)
        left(r.g_res.at[q, 0 : ns - 1], D + q)
        left(r.f_in.at[q, 0 : ns - 1], F + q)
        left(r.f_res.at[q, 0 : ns - 1], S + q)
        left(r.gx.at[q, 0 : (nh - 1) * rows, :], GX + q)
        left(r.gb.at[q, :, 0], GB2 + q)
        left(r.gc.at[q, :, 0], GC2 + q)
        left(r.gb_sum.at[q, 0 : chips - 1], GB + q)
        left(r.gc_sum.at[q, 0 : chips - 1], GC + q)
    for copy in own_gx + own_group:
        copy.wait()


def deliver(*refs):
    count = len(refs) // 2
    copies = [pltpu.make_async_copy(refs[i], refs[count + i], refs[-1].at[i]) for i in range(count)]
    for copy in copies:
        copy.start()
    for copy in copies:
        copy.wait()


def on_device(x_in, b_in, c_in, dt_in, a_log, skip_gain, grad_y):
    ns, nh = lax.axis_size("seq"), lax.axis_size("head")
    seqs, rows, all_heads = dt_in.shape
    heads = a_log.shape[0]
    width = heads * HEAD_DIM
    part = STATE // ns
    chips = nh // 2
    scratch = {
        "dt_pack": ((nh, rows, all_heads), BF16),
        "dt_all": ((nh, rows, all_heads), BF16),
        "c_all": ((seqs, chips, 2, rows, STATE), BF16),
        "b_all": ((seqs, chips, 2, rows, STATE), BF16),
        "x_all": ((seqs, nh, rows, width), BF16),
        "gy": ((seqs, STRETCH, width), BF16),
        "gy_t": ((seqs, width, STRETCH), BF16),
        "raw": ((seqs, STRETCH, LANES), F32),
        "dt": ((seqs, STRETCH, LANES), F32),
        "tot_send": ((8, LANES), F32),
        "tot_all": ((ns, 8, LANES), F32),
        "wide": ((ns * 8, width), F32),
        "own_wide": ((8, width), F32),
        "w_wide": ((seqs, STRETCH, width), F32),
        "e_wide": ((seqs, STRETCH, width), F32),
        "u_row": ((seqs, heads, STRETCH), F32),
        "cum_col": ((seqs, heads, STRETCH, LANES), F32),
        "gys_hi": ((seqs, STRETCH, width), BF16),
        "gys_lo": ((seqs, STRETCH, width), BF16),
        "xs_hi": ((seqs, STRETCH, width), BF16),
        "xs_lo": ((seqs, STRETCH, width), BF16),
        "scores": ((seqs, STRETCH, STRETCH), F32),
        "d_scores": ((seqs, STRETCH, STRETCH), F32),
        "decay": ((seqs, heads, STRETCH, STRETCH), F32),
        "mix_hi": ((seqs, heads, STRETCH, STRETCH), BF16),
        "mix_lo": ((seqs, heads, STRETCH, STRETCH), BF16),
        "z_t": ((seqs, width, STRETCH), F32),
        "xc": ((seqs, STRETCH, width), F32),
        "xp": ((seqs, STRETCH, width), F32),
        "y_in": ((seqs, STRETCH, width), F32),
        "gx": ((seqs, STRETCH, width), BF16),
        "gb": ((2 * seqs, chips, 2, rows, STATE), BF16),
        "gc": ((2 * seqs, chips, 2, rows, STATE), BF16),
        "gb_sum": ((seqs, chips, rows, STATE), BF16),
        "gc_sum": ((seqs, chips, rows, STATE), BF16),
        "gd_wide": ((seqs, STRETCH, LANES), F32),
        "gd": ((STRETCH, LANES), BF16),
        "gd_all": ((nh, rows, LANES), BF16),
    }
    for name in ("g", "f"):
        scratch[name + "_out"] = ((seqs, STATE, width), BF16)
        scratch[name + "_in"] = ((seqs, ns, part, width), BF16)
        scratch[name + "_res"] = ((seqs, ns, part, width), BF16)
    for name in ("d", "s"):
        scratch[name + "_all"] = ((seqs, STATE, width), F32)
        scratch[name + "_code"] = ((seqs, STATE, width), BF16)
        scratch[name + "_bound"] = ((seqs, ns, 1, width), F32)
    sems = 7 + 10 * seqs
    names = (
        ["a_log", "skip", "x_in", "b_in", "c_in", "dt_in", "gy_in"]
        + ["y_out", "gx_out", "gb_out", "gc_out", "gdt_out"]
        + list(scratch)
        + ["send_sem", "recv_sem", "local_sem"]
    )
    dims = (ns, nh, seqs, rows, heads)

    def body(*refs):
        mixer(dims, names, *refs)

    anywhere = pl.BlockSpec(memory_space=pl.ANY)
    small = pl.BlockSpec(memory_space=pltpu.SMEM)
    vmem = pl.BlockSpec(memory_space=pltpu.VMEM)

    def like(array):
        return jax.ShapeDtypeStruct(array.shape, BF16)

    results = pl.pallas_call(
        body,
        out_shape=tuple(pltpu.VMEM(array.shape, BF16) for array in (grad_y, x_in, b_in, c_in, dt_in)),
        in_specs=[small, small, anywhere, anywhere, anywhere, vmem, anywhere],
        out_specs=(vmem,) * 5,
        scratch_shapes=[pltpu.VMEM(shape, dtype) for shape, dtype in scratch.values()]
        + [
            pltpu.SemaphoreType.DMA((sems,)),
            pltpu.SemaphoreType.DMA((sems,)),
            pltpu.SemaphoreType.DMA((4 + 3 * seqs,)),
        ],
        compiler_params=pltpu.CompilerParams(
            collective_id=0, has_side_effects=True, vmem_limit_bytes=56 * 1024 * 1024
        ),
        name="mixer",
    )(a_log, skip_gain, x_in, b_in, c_in, dt_in, grad_y)
    results = [pltpu.with_memory_space_constraint(result, pltpu.VMEM) for result in results]
    return pl.pallas_call(
        deliver,
        out_shape=tuple(like(result) for result in results),
        in_specs=[anywhere] * len(results),
        out_specs=(anywhere,) * len(results),
        scratch_shapes=[pltpu.SemaphoreType.DMA((len(results),))],
        name="deliver",
    )(*results)


def solution(mesh):
    spread = P(None, ("seq", "head"), None)
    return jax.shard_map(
        on_device,
        mesh=mesh,
        in_specs=(spread, spread, spread, spread, P("head"), P("head"), P(None, "seq", "head")),
        out_specs=(P(None, "seq", "head"), spread, spread, spread, spread),
        check_vma=False,
    )
```

```python
from types import SimpleNamespace

import jax
import jax.numpy as jnp
from jax import lax
from jax.experimental import pallas as pl
from jax.experimental.pallas import tpu as pltpu
from jax.sharding import PartitionSpec as P

HEAD_DIM = 64
STATE = 256
STRETCH = 256
LANES = 128
MESH = pl.DeviceIdType.MESH
F32 = jnp.float32
BF16 = jnp.bfloat16
NN = (((1,), (0,)), ((), ()))
NT = (((1,), (1,)), ((), ()))
TN = (((0,), (0,)), ((), ()))
LN2 = 0.6931471805599453
TINY = 1e-30
CODE_SPAN = 252.0
X_B = 6.0 * 6.0 * 1.001
GY_C = 4.0 * 0.375 * 1.001


def dot(a, b, dims=NN):
    return lax.dot_general(a, b, dims, preferred_element_type=F32)


def split(value, count):
    parts = []
    for _ in range(count):
        part = value.astype(BF16)
        parts.append(part)
        value = value - part.astype(F32)
    return parts


def dot_split(a, b, dims=NN):
    a_parts = [a] if a.dtype == BF16 else split(a, 2)
    b_parts = [b] if b.dtype == BF16 else split(b, 2)
    total = dot(a_parts[0], b_parts[0], dims)
    for i, left in enumerate(a_parts):
        for j, right in enumerate(b_parts):
            if i + j == 1:
                total = total + dot(left, right, dims)
    return total


def times_exact(value, ones):
    first, second, third = split(value, 3)
    return dot(first, ones) + (dot(second, ones) + dot(third, ones))


def exact_times(ones, value):
    first, second, third = split(value, 3)
    return dot(ones, first) + (dot(ones, second) + dot(ones, third))


def encode(value, bound):
    share = jnp.maximum(jnp.abs(value) / jnp.maximum(bound, TINY), TINY)
    level = jnp.exp2(jnp.log(share) * (0.125 / LN2))
    code = jnp.exp2(level * CODE_SPAN - 0.5 * CODE_SPAN)
    return jnp.where(value < 0.0, -code, code).astype(BF16)


def decode(code, bound):
    code = code.astype(F32)
    level = jnp.maximum(jnp.log(jnp.abs(code)) * (1.0 / (LN2 * CODE_SPAN)) + 0.5, 0.0)
    square = level * level
    square = square * square
    size = square * square * bound
    return jnp.where(code < 0.0, -size, size)


def iota(shape, axis):
    return lax.broadcasted_iota(jnp.int32, shape, axis)


def one_hot(condition):
    return jnp.where(condition, 1.0, 0.0).astype(BF16)


def mixer(dims, names, *refs):
    r = SimpleNamespace(**dict(zip(names, refs)))
    ns, nh, seqs, rows, heads = dims
    width = heads * HEAD_DIM
    part = STATE // ns
    chips = nh // 2
    s, h = lax.axis_index("seq"), lax.axis_index("head")
    core = lax.rem(h, 2)
    chip = h // 2
    other = (s, h + 1 - 2 * core)

    def out_and_in(i, count):
        return count // 2 + (2 * (i % 2) - 1) * ((i + 1) // 2)

    def head_peer(i):
        return lax.rem(h + out_and_in(i, nh), nh)

    def same_core_peer(i):
        return lax.rem(h + 2 * out_and_in(i, chips), nh)

    def seq_peer(i):
        return lax.rem(s + 1 + i, ns)

    def remote(src, dst, sem, device):
        pltpu.make_async_remote_copy(
            src, dst, r.send_sem.at[sem], r.recv_sem.at[sem], device_id=device, device_id_type=MESH
        ).start()

    def local(src, dst, sem):
        copy = pltpu.make_async_copy(src, dst, r.local_sem.at[sem])
        copy.start()
        return copy

    def arrived(ref, sem):
        pltpu.make_async_copy(ref, ref, r.recv_sem.at[sem]).wait()

    def left(ref, sem):
        pltpu.make_async_copy(ref, ref, r.send_sem.at[sem]).wait()

    def over(count, body):
        def one(i, carry):
            body(i)
            return carry

        lax.fori_loop(0, count, one, 0)

    def columns(index, size):
        return pl.ds(pl.multiple_of(index * size, size), size)

    DT, C, C2, B, B2, TOT, GD = range(7)
    X, G, D, F, S, GX, GB, GC, GB2, GC2 = (7 + seqs * i for i in range(10))

    barrier = pltpu.get_barrier_semaphore()

    def greet_head(k):
        pl.semaphore_signal(barrier, inc=1, device_id=(s, head_peer(k)), device_id_type=MESH)

    def greet_seq(k):
        pl.semaphore_signal(barrier, inc=1, device_id=(seq_peer(k), h), device_id_type=MESH)

    over(nh - 1, greet_head)
    over(ns - 1, greet_seq)

    own = [
        local(r.c_in.at[:, :, columns(chip, STATE)], r.c_all.at[:, chip, core], 0),
        local(r.b_in.at[:, :, columns(chip, STATE)], r.b_all.at[:, chip, core], 1),
        local(r.x_in.at[:, :, columns(h, width)], r.x_all.at[:, h], 2),
        local(r.gy_in, r.gy, 3),
    ]

    lane_at = iota((nh, LANES), 1)
    group_at = lane_at // heads == iota((nh, LANES), 0)
    regroup_at = (nh * LANES, LANES)
    r.regroup[...] = one_hot(
        (iota(regroup_at, 1) // heads == iota(regroup_at, 0) // LANES)
        & (iota(regroup_at, 1) % heads == iota(regroup_at, 0) % heads)
    )

    def regrouped(row_of):
        return dot(
            jnp.concatenate(
                [jnp.where(group_at, row_of(i), 0.0).astype(BF16) for i in range(nh)], axis=1
            ),
            r.regroup[...],
        )

    for q in range(seqs):
        raw = r.dt_in[q].astype(F32)
        packed = regrouped(lambda i, raw=raw: raw[i : i + 1, :])
        for p in range(nh):
            r.dt_pack[p, :, q * LANES : (q + 1) * LANES] = packed[p : p + 1, :]
    r.dt_all[h] = r.dt_pack[h]
    own[3].wait()
    for q in range(seqs):
        r.gy_t[q] = jnp.transpose(r.gy[q])

    pl.semaphore_wait(barrier, nh - 1 + ns - 1)

    def send_dt(k):
        peer = head_peer(k)
        remote(r.dt_pack.at[peer], r.dt_all.at[h], DT, (s, peer))

    def send_c(k):
        peer = same_core_peer(k)
        remote(r.c_in.at[:, :, columns(peer // 2, STATE)], r.c_all.at[:, chip, core], C, (s, peer))

    def send_b(k):
        peer = same_core_peer(k)
        remote(r.b_in.at[:, :, columns(peer // 2, STATE)], r.b_all.at[:, chip, core], B, (s, peer))

    over(nh - 1, send_dt)
    over(chips - 1, send_c)
    over(chips - 1, send_b)
    for q in range(seqs):

        def send_x(k, q=q):
            peer = head_peer(k)
            remote(r.x_in.at[q, :, columns(peer, width)], r.x_all.at[q, h], X + q, (s, peer))

        over(nh - 1, send_x)

    lane_row = iota((1, LANES), 1)
    rate = jnp.zeros((1, LANES), F32)
    skip_row = jnp.zeros((1, width), F32)
    wide_row = iota((1, width), 1) // HEAD_DIM
    for e in range(heads):
        rate = jnp.where(lane_row == e, r.a_log[e], rate)
        skip_row = jnp.where(wide_row == e, r.skip[e], skip_row)
    rate = jnp.where(lane_row < heads, -jnp.exp(rate), 0.0)
    spread = one_hot(iota((LANES, width), 0) == iota((LANES, width), 1) // HEAD_DIM)
    gather = one_hot(iota((width, LANES), 0) // HEAD_DIM == iota((width, LANES), 1))
    causal = iota((STRETCH, STRETCH), 0) >= iota((STRETCH, STRETCH), 1)
    lower = one_hot(causal)
    upper = one_hot(iota((STRETCH, STRETCH), 0) <= iota((STRETCH, STRETCH), 1))

    arrived(r.dt_all.at[0 : nh - 1], DT)
    token_lane = iota((STRETCH, LANES), 1) // heads == iota((STRETCH, LANES), 0) % rows
    head_of_lane = iota((LANES, LANES), 0) % heads == iota((LANES, LANES), 1)
    lane_of_head = iota((LANES, LANES), 1) % heads == iota((LANES, LANES), 0)
    r.tot_send[...] = jnp.zeros_like(r.tot_send)
    for q in range(seqs):
        by_device = jnp.concatenate(
            [
                jnp.broadcast_to(r.dt_all[p, :, q * LANES : (q + 1) * LANES], (rows, LANES))
                for p in range(nh)
            ],
            axis=0,
        )
        raw = dot(jnp.where(token_lane, by_device, 0.0).astype(BF16), one_hot(head_of_lane))
        dt = jnp.maximum(raw, 0.0) + jnp.log1p(jnp.exp(-jnp.abs(raw)))
        cum = exact_times(lower, dt * rate)
        last = cum[STRETCH - 1 :, :]
        r.raw[q] = raw
        r.dt[q] = dt
        weight = jnp.exp(last - cum) * dt
        growth = jnp.exp(cum)
        r.tot_send[pl.ds(q, 1), :] = last
        r.tot_send[pl.ds(seqs + q, 1), :] = X_B * jnp.sum(weight, axis=0, keepdims=True)
        r.tot_send[pl.ds(2 * seqs + q, 1), :] = GY_C * jnp.sum(growth, axis=0, keepdims=True)
        r.weight[q] = weight
        r.cum[q] = cum
        r.e_wide[q] = times_exact(growth, spread)

    def send_tot(k):
        remote(r.tot_send, r.tot_all.at[s], TOT, (seq_peer(k), h))

    over(ns - 1, send_tot)
    r.tot_all[s] = r.tot_send[...]
    r.own_wide[...] = times_exact(r.tot_send[...], spread)

    def own_bound(row):
        return r.own_wide[pl.ds(row, 1), :]

    own[0].wait()
    arrived(r.c_all.at[:, 0 : chips - 1, 0], C)
    remote(r.c_all.at[:, :, core], r.c_all.at[:, :, core], C2, other)
    for q in range(seqs):
        first, second = split(r.gy[q].astype(F32) * r.e_wide[q], 2)
        r.gys_hi[q] = first
        r.gys_lo[q] = second
    arrived(r.c_all.at[:, :, 0], C2)

    def c_of(q):
        return r.c_all[q].reshape(STRETCH, STATE)

    def b_of(q):
        return r.b_all[q].reshape(STRETCH, STATE)

    def x_of(q):
        return r.x_all[q].reshape(STRETCH, width)

    def send_parts(q, source, target, sem):
        def one(k):
            peer = seq_peer(k)
            remote(source.at[q, columns(peer, part), :], target.at[q, s], sem + q, (peer, h))

        over(ns - 1, one)
        target[q, s] = source[q, columns(s, part), :]

    for q in range(seqs):
        state = dot(c_of(q), r.gys_hi[q], TN) + dot(c_of(q), r.gys_lo[q], TN)
        r.g_out[q] = encode(state, own_bound(2 * seqs + q))
        send_parts(q, r.g_out, r.g_in, G)

    for q in range(seqs):
        cum = r.cum[q]
        r.w_wide[q] = times_exact(r.weight[q], spread)
        r.u_row[q] = jnp.transpose(cum - jnp.log(r.dt[q]))[:heads, :]
        for e in range(heads):
            r.cum_col[q, e] = jnp.broadcast_to(cum[:, e : e + 1], (STRETCH, LANES))

    own[1].wait()
    arrived(r.b_all.at[:, 0 : chips - 1, 0], B)
    remote(r.b_all.at[:, :, core], r.b_all.at[:, :, core], B2, other)
    arrived(r.b_all.at[:, :, 0], B2)

    def decays(q):
        r.scores[q] = dot(c_of(q), b_of(q), NT)

        def one(e):
            column = r.cum_col[q, e]
            gap = jnp.concatenate([column, column], axis=1) - r.u_row[q, pl.ds(e, 1), :]
            decay = jnp.where(causal, jnp.exp(gap), 0.0)
            r.decay[q, e] = decay
            first, second = split(r.scores[q] * decay, 2)
            r.mix_hi[q, e] = first
            r.mix_lo[q, e] = second
            rows_e = columns(e, HEAD_DIM)
            grad = r.gy_t[q, rows_e, :]
            r.z_t[q, rows_e, :] = dot(grad, first) + dot(grad, second)

        over(heads, one)

    def send_state(q):
        arrived(r.x_all.at[q, 0 : nh - 1], X + q)
        first, second = split(x_of(q).astype(F32) * r.w_wide[q], 2)
        r.xs_hi[q] = first
        r.xs_lo[q] = second
        state = dot(b_of(q), first, TN) + dot(b_of(q), second, TN)
        r.f_out[q] = encode(state, own_bound(seqs + q))
        send_parts(q, r.f_out, r.f_in, F)

    def within(q):
        r.d_scores[q] = jnp.zeros((STRETCH, STRETCH), F32)
        low = iota((STRETCH, LANES), 1) < HEAD_DIM

        def one(i):
            cols = columns(i, LANES)
            x_pair = r.x_all[q, :, :, cols].reshape(STRETCH, LANES)
            grad = r.gy[q, :, cols].astype(F32)
            results = []
            total = r.d_scores[q]
            for k in range(2):
                e = 2 * i + k
                results.append(dot(r.mix_hi[q, e], x_pair) + dot(r.mix_lo[q, e], x_pair))
                masked = jnp.where(low if k == 0 else ~low, grad, 0.0).astype(BF16)
                total = total + dot(masked, x_pair, NT) * r.decay[q, e]
            r.d_scores[q] = total
            r.y_in[q, :, cols] = jnp.where(low, results[0], results[1])

        over(heads // 2, one)

    def scan(q, source, result, bounds, target, sem, sem_in, bound_row, reverse):
        arrived(source.at[q, 0 : ns - 1], sem_in + q)

        def wide(block, row):
            return r.wide[pl.ds(block * 8 + row, 1), :]

        def one(i, carry):
            block = ns - 1 - i if reverse else i
            state, bound = carry
            bounds[q, block] = bound
            result[q, block] = encode(state, bound)
            factor = jnp.exp(wide(block, q))
            block_bound = wide(block, bound_row + q)
            return (factor * state + decode(source[q, block], block_bound), factor * bound + block_bound)

        lax.fori_loop(0, ns, one, (jnp.zeros((part, width), F32), jnp.zeros((1, width), F32)), unroll=4)

        def back(k):
            peer = seq_peer(k)
            remote(result.at[q, peer], target.at[q, columns(s, part), :], sem + q, (peer, h))

        over(ns - 1, back)
        target[q, columns(s, part), :] = result[q, s]

    def scan_back(q):
        scan(q, r.g_in, r.g_res, r.d_bound, r.d_code, D, G, 2 * seqs, True)

    def scan_on(q):
        scan(q, r.f_in, r.f_res, r.s_bound, r.s_code, S, F, seqs, False)

    def states_here(q, codes, bounds, target, sem):
        arrived(codes.at[q, 0 : (ns - 1) * part, :], sem + q)
        target[q] = decode(codes[q], bounds[q, s])

    def send_rows(q, source, target_of, sem):
        def one(k):
            peer = head_peer(k)
            remote(source.at[q, columns(peer, rows), :], target_of(q), sem + q, (s, peer))

        over(nh - 1, one)

    def gx_slot(q):
        return r.gx_out.at[q, :, columns(h, width)]

    own_gx = []

    def grad_x(q):
        states_here(q, r.d_code, r.d_bound, r.d_all, D)
        r.xc[q] = r.w_wide[q] * dot_split(b_of(q), r.d_all[q])
        r.xp[q] = jnp.transpose(r.z_t[q]) + r.xc[q]
        r.gx[q] = (skip_row * r.gy[q].astype(F32) + r.xp[q]).astype(BF16)
        send_rows(q, r.gx, gx_slot, GX)
        own_gx.append(local(r.gx.at[q, columns(h, rows), :], gx_slot(q), 4 + q))

    def hand_over(q, value, slices, sem):
        slices[q] = value.astype(BF16).reshape(chips, 2, rows, STATE)
        remote(slices.at[q, :, 1 - core], slices.at[seqs + q, :, 0], sem + q, other)

    own_group = []

    def join(q, slices, sums, out, sem_in, sem, number):
        arrived(slices.at[seqs + q, :, 0], sem_in + q)
        sums[q] = (slices[q, :, core].astype(F32) + slices[seqs + q, :, 0].astype(F32)).astype(BF16)

        def slot():
            return out.at[q, :, columns(chip, STATE)]

        def one(k):
            peer = same_core_peer(k)
            remote(sums.at[q, peer // 2], slot(), sem + q, (s, peer))

        over(chips - 1, one)
        own_group.append(local(sums.at[q, chip], slot(), number))

    def grad_b(q):
        first, second = split(jnp.transpose(r.d_scores[q]), 2)
        value = dot(first, c_of(q)) + dot(second, c_of(q))
        d_hi, d_lo = split(r.d_all[q], 2)
        value = value + dot(r.xs_hi[q], d_hi, NT)
        value = value + (dot(r.xs_hi[q], d_lo, NT) + dot(r.xs_lo[q], d_hi, NT))
        hand_over(q, value, r.gb, GB2)

    def join_b(q):
        join(q, r.gb, r.gb_sum, r.gb_out, GB2, GB, 4 + seqs + q)

    def join_c(q):
        join(q, r.gc, r.gc_sum, r.gc_out, GC2, GC, 4 + 2 * seqs + q)

    def grad_c(q):
        states_here(q, r.s_code, r.s_bound, r.s_all, S)
        s_hi, s_lo = split(r.s_all[q], 2)
        first, second = split(r.d_scores[q], 2)
        value = dot(first, b_of(q)) + dot(second, b_of(q))
        value = value + dot(r.gys_hi[q], s_hi, NT)
        value = value + (dot(r.gys_hi[q], s_lo, NT) + dot(r.gys_lo[q], s_hi, NT))
        hand_over(q, value, r.gc, GC2)

    def outputs(q):
        y = r.y_in[q] + r.e_wide[q] * dot_split(c_of(q), r.s_all[q])
        x = x_of(q).astype(F32)
        r.y_out[q] = (y + skip_row * x).astype(BF16)

        dt = r.dt[q]
        v = times_exact(x * r.xp[q], gather)
        d_cum = times_exact(r.gy[q].astype(F32) * y, gather) - v
        at_last = jnp.sum(x * r.xc[q], axis=0, keepdims=True) + r.e_wide[q, STRETCH - 1 :, :] * jnp.sum(
            r.s_all[q] * r.d_all[q], axis=0, keepdims=True
        )
        at_last = times_exact(jnp.broadcast_to(at_last, (8, width)), gather)[:1]
        d_sum = exact_times(upper, d_cum) + at_last
        r.gd_wide[q] = (v / dt + rate * d_sum) * jax.nn.sigmoid(r.raw[q])

    def send_steps():
        for q in range(seqs):
            values = dot(r.gd_wide[q].astype(BF16), one_hot(lane_of_head))
            values = jnp.where(token_lane, values, 0.0).reshape(nh, rows, LANES).sum(axis=1)
            for p in range(nh):
                r.gd_pack[p, :, q * LANES : (q + 1) * LANES] = values[p : p + 1, :]

        def one(k):
            peer = head_peer(k)
            remote(r.gd_pack.at[peer], r.gd_all.at[h], GD, (s, peer))

        over(nh - 1, one)
        r.gd_all[h] = r.gd_pack[h]

    decays(0)
    arrived(r.tot_all.at[0 : ns - 1], TOT)
    r.wide[...] = times_exact(r.tot_all[...].reshape(ns * 8, LANES), spread)
    scan_back(0)
    scan_back(1)
    own[2].wait()
    send_state(0)
    decays(1)
    send_state(1)
    grad_x(0)
    grad_x(1)
    within(0)
    scan_on(0)
    within(1)
    scan_on(1)
    grad_b(0)
    grad_b(1)
    join_b(0)
    join_b(1)
    grad_c(0)
    outputs(0)
    join_c(0)
    grad_c(1)
    outputs(1)
    send_steps()
    join_c(1)

    arrived(r.gd_all.at[0 : nh - 1], GD)
    for q in range(seqs):
        r.gdt_out[q] = regrouped(lambda i, q=q: r.gd_all[i, :, q * LANES : (q + 1) * LANES]).astype(BF16)
    for q in range(seqs):
        arrived(r.gx_out.at[q, :, 0 : (nh - 1) * width], GX + q)
        arrived(r.gb_out.at[q, :, 0 : (chips - 1) * STATE], GB + q)
        arrived(r.gc_out.at[q, :, 0 : (chips - 1) * STATE], GC + q)

    left(r.dt_all.at[0 : nh - 1], DT)
    left(r.gd_all.at[0 : nh - 1], GD)
    left(r.c_all.at[:, 0 : chips - 1, 0], C)
    left(r.c_all.at[:, :, 0], C2)
    left(r.b_all.at[:, 0 : chips - 1, 0], B)
    left(r.b_all.at[:, :, 0], B2)
    left(r.tot_all.at[0 : ns - 1], TOT)
    for q in range(seqs):
        left(r.x_all.at[q, 0 : nh - 1], X + q)
        left(r.g_in.at[q, 0 : ns - 1], G + q)
        left(r.g_res.at[q, 0 : ns - 1], D + q)
        left(r.f_in.at[q, 0 : ns - 1], F + q)
        left(r.f_res.at[q, 0 : ns - 1], S + q)
        left(r.gx.at[q, 0 : (nh - 1) * rows, :], GX + q)
        left(r.gb.at[q, :, 0], GB2 + q)
        left(r.gc.at[q, :, 0], GC2 + q)
        left(r.gb_sum.at[q, 0 : chips - 1], GB + q)
        left(r.gc_sum.at[q, 0 : chips - 1], GC + q)
    for copy in own_gx + own_group:
        copy.wait()


def deliver(*refs):
    count = len(refs) // 2
    copies = [pltpu.make_async_copy(refs[i], refs[count + i], refs[-1].at[i]) for i in range(count)]
    for copy in copies:
        copy.start()
    for copy in copies:
        copy.wait()


def on_device(x_in, b_in, c_in, dt_in, a_log, skip_gain, grad_y):
    ns, nh = lax.axis_size("seq"), lax.axis_size("head")
    seqs, rows, all_heads = dt_in.shape
    heads = a_log.shape[0]
    width = heads * HEAD_DIM
    part = STATE // ns
    chips = nh // 2
    scratch = {
        "regroup": ((nh * LANES, LANES), BF16),
        "dt_pack": ((nh, 1, seqs * LANES), F32),
        "dt_all": ((nh, 1, seqs * LANES), F32),
        "c_all": ((seqs, chips, 2, rows, STATE), BF16),
        "b_all": ((seqs, chips, 2, rows, STATE), BF16),
        "x_all": ((seqs, nh, rows, width), BF16),
        "gy": ((seqs, STRETCH, width), BF16),
        "gy_t": ((seqs, width, STRETCH), BF16),
        "raw": ((seqs, STRETCH, LANES), F32),
        "dt": ((seqs, STRETCH, LANES), F32),
        "weight": ((seqs, STRETCH, LANES), F32),
        "cum": ((seqs, STRETCH, LANES), F32),
        "tot_send": ((8, LANES), F32),
        "tot_all": ((ns, 8, LANES), F32),
        "wide": ((ns * 8, width), F32),
        "own_wide": ((8, width), F32),
        "w_wide": ((seqs, STRETCH, width), F32),
        "e_wide": ((seqs, STRETCH, width), F32),
        "u_row": ((seqs, heads, STRETCH), F32),
        "cum_col": ((seqs, heads, STRETCH, LANES), F32),
        "gys_hi": ((seqs, STRETCH, width), BF16),
        "gys_lo": ((seqs, STRETCH, width), BF16),
        "xs_hi": ((seqs, STRETCH, width), BF16),
        "xs_lo": ((seqs, STRETCH, width), BF16),
        "scores": ((seqs, STRETCH, STRETCH), F32),
        "d_scores": ((seqs, STRETCH, STRETCH), F32),
        "decay": ((seqs, heads, STRETCH, STRETCH), F32),
        "mix_hi": ((seqs, heads, STRETCH, STRETCH), BF16),
        "mix_lo": ((seqs, heads, STRETCH, STRETCH), BF16),
        "z_t": ((seqs, width, STRETCH), F32),
        "xc": ((seqs, STRETCH, width), F32),
        "xp": ((seqs, STRETCH, width), F32),
        "y_in": ((seqs, STRETCH, width), F32),
        "gx": ((seqs, STRETCH, width), BF16),
        "gb": ((2 * seqs, chips, 2, rows, STATE), BF16),
        "gc": ((2 * seqs, chips, 2, rows, STATE), BF16),
        "gb_sum": ((seqs, chips, rows, STATE), BF16),
        "gc_sum": ((seqs, chips, rows, STATE), BF16),
        "gd_wide": ((seqs, STRETCH, LANES), F32),
        "gd_pack": ((nh, 1, seqs * LANES), F32),
        "gd_all": ((nh, 1, seqs * LANES), F32),
    }
    for name in ("g", "f"):
        scratch[name + "_out"] = ((seqs, STATE, width), BF16)
        scratch[name + "_in"] = ((seqs, ns, part, width), BF16)
        scratch[name + "_res"] = ((seqs, ns, part, width), BF16)
    for name in ("d", "s"):
        scratch[name + "_all"] = ((seqs, STATE, width), F32)
        scratch[name + "_code"] = ((seqs, STATE, width), BF16)
        scratch[name + "_bound"] = ((seqs, ns, 1, width), F32)
    sems = 7 + 10 * seqs
    names = (
        ["a_log", "skip", "x_in", "b_in", "c_in", "dt_in", "gy_in"]
        + ["y_out", "gx_out", "gb_out", "gc_out", "gdt_out"]
        + list(scratch)
        + ["send_sem", "recv_sem", "local_sem"]
    )
    dims = (ns, nh, seqs, rows, heads)

    def body(*refs):
        mixer(dims, names, *refs)

    anywhere = pl.BlockSpec(memory_space=pl.ANY)
    small = pl.BlockSpec(memory_space=pltpu.SMEM)
    vmem = pl.BlockSpec(memory_space=pltpu.VMEM)

    def like(array):
        return jax.ShapeDtypeStruct(array.shape, BF16)

    results = pl.pallas_call(
        body,
        out_shape=tuple(pltpu.VMEM(array.shape, BF16) for array in (grad_y, x_in, b_in, c_in, dt_in)),
        in_specs=[small, small, anywhere, anywhere, anywhere, vmem, anywhere],
        out_specs=(vmem,) * 5,
        scratch_shapes=[pltpu.VMEM(shape, dtype) for shape, dtype in scratch.values()]
        + [
            pltpu.SemaphoreType.DMA((sems,)),
            pltpu.SemaphoreType.DMA((sems,)),
            pltpu.SemaphoreType.DMA((4 + 3 * seqs,)),
        ],
        compiler_params=pltpu.CompilerParams(
            collective_id=0, has_side_effects=True, vmem_limit_bytes=56 * 1024 * 1024
        ),
        name="mixer",
    )(a_log, skip_gain, x_in, b_in, c_in, dt_in, grad_y)
    results = [pltpu.with_memory_space_constraint(result, pltpu.VMEM) for result in results]
    return pl.pallas_call(
        deliver,
        out_shape=tuple(like(result) for result in results),
        in_specs=[anywhere] * len(results),
        out_specs=(anywhere,) * len(results),
        scratch_shapes=[pltpu.SemaphoreType.DMA((len(results),))],
        name="deliver",
    )(*results)


def solution(mesh):
    spread = P(None, ("seq", "head"), None)
    return jax.shard_map(
        on_device,
        mesh=mesh,
        in_specs=(spread, spread, spread, spread, P("head"), P("head"), P(None, "seq", "head")),
        out_specs=(P(None, "seq", "head"), spread, spread, spread, spread),
        check_vma=False,
    )
```

```python
from types import SimpleNamespace

import jax
import jax.numpy as jnp
from jax import lax
from jax.experimental import pallas as pl
from jax.experimental.pallas import tpu as pltpu
from jax.sharding import PartitionSpec as P

HEAD_DIM = 64
STATE = 256
STRETCH = 256
CUTS = 1
LANES = 128
MESH = pl.DeviceIdType.MESH
F32 = jnp.float32
BF16 = jnp.bfloat16
NN = (((1,), (0,)), ((), ()))
NT = (((1,), (1,)), ((), ()))
TN = (((0,), (0,)), ((), ()))
LN2 = 0.6931471805599453
TINY = 1e-30
CODE_SPAN = 252.0
X_B = 6.0 * 6.0 * 1.001
GY_C = 4.0 * 0.375 * 1.001


def dot(a, b, dims=NN):
    return lax.dot_general(a, b, dims, preferred_element_type=F32)


def split(value, count):
    parts = []
    for _ in range(count):
        part = value.astype(BF16)
        parts.append(part)
        value = value - part.astype(F32)
    return parts


def dot_split(a, b, dims=NN):
    a_parts = [a] if a.dtype == BF16 else split(a, 2)
    b_parts = [b] if b.dtype == BF16 else split(b, 2)
    total = dot(a_parts[0], b_parts[0], dims)
    for i, left in enumerate(a_parts):
        for j, right in enumerate(b_parts):
            if i + j == 1:
                total = total + dot(left, right, dims)
    return total


def times_exact(value, ones):
    first, second, third = split(value, 3)
    return dot(first, ones) + (dot(second, ones) + dot(third, ones))


def exact_times(ones, value):
    first, second, third = split(value, 3)
    return dot(ones, first) + (dot(ones, second) + dot(ones, third))


def encode(value, bound):
    share = jnp.maximum(jnp.abs(value) * (1.0 / jnp.maximum(bound, TINY)), TINY)
    level = jnp.exp2(jnp.log(share) * (0.125 / LN2))
    code = jnp.exp2(level * CODE_SPAN - 0.5 * CODE_SPAN)
    return jnp.where(value < 0.0, -code, code).astype(BF16)


def decode(code, bound):
    code = code.astype(F32)
    level = jnp.maximum(jnp.log(jnp.abs(code)) * (1.0 / (LN2 * CODE_SPAN)) + 0.5, 0.0)
    square = level * level
    square = square * square
    size = square * square * bound
    return jnp.where(code < 0.0, -size, size)


def iota(shape, axis):
    return lax.broadcasted_iota(jnp.int32, shape, axis)


def one_hot(condition):
    return jnp.where(condition, 1.0, 0.0).astype(BF16)


def mixer(dims, names, *refs):
    r = SimpleNamespace(**dict(zip(names, refs)))
    ns, nh, seqs, rows, heads = dims
    width = heads * HEAD_DIM
    part = STATE // ns
    chips = nh // 2
    half = width // CUTS
    s, h = lax.axis_index("seq"), lax.axis_index("head")
    core = lax.rem(h, 2)
    chip = h // 2
    other = (s, h + 1 - 2 * core)

    def out_and_in(i, count):
        return count // 2 + (2 * (i % 2) - 1) * ((i + 1) // 2)

    def head_peer(i):
        return lax.rem(h + out_and_in(i, nh), nh)

    def same_core_peer(i):
        return lax.rem(h + 2 * out_and_in(i, chips), nh)

    def seq_peer(i):
        return lax.rem(s + 1 + i, ns)

    def remote(src, dst, sem, device):
        pltpu.make_async_remote_copy(
            src, dst, r.send_sem.at[sem], r.recv_sem.at[sem], device_id=device, device_id_type=MESH
        ).start()

    def local(src, dst, sem):
        copy = pltpu.make_async_copy(src, dst, r.local_sem.at[sem])
        copy.start()
        return copy

    def arrived(ref, sem):
        pltpu.make_async_copy(ref, ref, r.recv_sem.at[sem]).wait()

    def left(ref, sem):
        pltpu.make_async_copy(ref, ref, r.send_sem.at[sem]).wait()

    def over(count, body):
        def one(i, carry):
            body(i)
            return carry

        lax.fori_loop(0, count, one, 0)

    def columns(index, size):
        return pl.ds(pl.multiple_of(index * size, size), size)

    DT, C, C2, B, B2, TOT, GD = range(7)
    X, F, S, GX, GB, GC, GB2, GC2 = (7 + seqs * i for i in range(8))
    G, D = (7 + seqs * (8 + CUTS * i) for i in range(2))

    barrier = pltpu.get_barrier_semaphore()

    def greet_head(k):
        pl.semaphore_signal(barrier, inc=1, device_id=(s, head_peer(k)), device_id_type=MESH)

    def greet_seq(k):
        pl.semaphore_signal(barrier, inc=1, device_id=(seq_peer(k), h), device_id_type=MESH)

    over(nh - 1, greet_head)
    over(ns - 1, greet_seq)

    own = [
        local(r.c_in.at[:, :, columns(chip, STATE)], r.c_all.at[:, chip, core], 0),
        local(r.b_in.at[:, :, columns(chip, STATE)], r.b_all.at[:, chip, core], 1),
        local(r.x_in.at[:, :, columns(h, width)], r.x_all.at[:, h], 2),
        local(r.gy_in, r.gy, 3),
    ]

    lane_at = iota((nh, LANES), 1)
    group_at = lane_at // heads == iota((nh, LANES), 0)
    regroup_at = (nh * LANES, LANES)
    r.regroup[...] = one_hot(
        (iota(regroup_at, 1) // heads == iota(regroup_at, 0) // LANES)
        & (iota(regroup_at, 1) % heads == iota(regroup_at, 0) % heads)
    )

    def regrouped(row_of):
        return dot(
            jnp.concatenate(
                [jnp.where(group_at, row_of(i), 0.0).astype(BF16) for i in range(nh)], axis=1
            ),
            r.regroup[...],
        )

    for q in range(seqs):
        raw = r.dt_in[q].astype(F32)
        packed = regrouped(lambda i, raw=raw: raw[i : i + 1, :])
        for p in range(nh):
            r.dt_pack[p, :, q * LANES : (q + 1) * LANES] = packed[p : p + 1, :]
    r.dt_all[h] = r.dt_pack[h]
    own[3].wait()
    for q in range(seqs):
        r.gy_t[q] = jnp.transpose(r.gy[q])

    pl.semaphore_wait(barrier, nh - 1 + ns - 1)

    def send_dt(k):
        peer = head_peer(k)
        remote(r.dt_pack.at[peer], r.dt_all.at[h], DT, (s, peer))

    def send_c(k):
        peer = same_core_peer(k)
        remote(r.c_in.at[:, :, columns(peer // 2, STATE)], r.c_all.at[:, chip, core], C, (s, peer))

    def send_b(k):
        peer = same_core_peer(k)
        remote(r.b_in.at[:, :, columns(peer // 2, STATE)], r.b_all.at[:, chip, core], B, (s, peer))

    over(nh - 1, send_dt)
    over(chips - 1, send_c)
    over(chips - 1, send_b)
    for q in range(seqs):

        def send_x(k, q=q):
            peer = head_peer(k)
            remote(r.x_in.at[q, :, columns(peer, width)], r.x_all.at[q, h], X + q, (s, peer))

        over(nh - 1, send_x)

    lane_row = iota((1, LANES), 1)
    rate = jnp.zeros((1, LANES), F32)
    skip_row = jnp.zeros((1, width), F32)
    wide_row = iota((1, width), 1) // HEAD_DIM
    for e in range(heads):
        rate = jnp.where(lane_row == e, r.a_log[e], rate)
        skip_row = jnp.where(wide_row == e, r.skip[e], skip_row)
    rate = jnp.where(lane_row < heads, -jnp.exp(rate), 0.0)
    spread = one_hot(iota((LANES, width), 0) == iota((LANES, width), 1) // HEAD_DIM)
    gather = one_hot(iota((width, LANES), 0) // HEAD_DIM == iota((width, LANES), 1))
    causal = iota((STRETCH, STRETCH), 0) >= iota((STRETCH, STRETCH), 1)
    lower = one_hot(causal)
    upper = one_hot(iota((STRETCH, STRETCH), 0) <= iota((STRETCH, STRETCH), 1))

    arrived(r.dt_all.at[0 : nh - 1], DT)
    token_lane = iota((STRETCH, LANES), 1) // heads == iota((STRETCH, LANES), 0) % rows
    head_of_lane = iota((LANES, LANES), 0) % heads == iota((LANES, LANES), 1)
    lane_of_head = iota((LANES, LANES), 1) % heads == iota((LANES, LANES), 0)
    r.tot_send[...] = jnp.zeros_like(r.tot_send)
    for q in range(seqs):
        by_device = jnp.concatenate(
            [
                jnp.broadcast_to(r.dt_all[p, :, q * LANES : (q + 1) * LANES], (rows, LANES))
                for p in range(nh)
            ],
            axis=0,
        )
        raw = dot(jnp.where(token_lane, by_device, 0.0).astype(BF16), one_hot(head_of_lane))
        dt = jnp.maximum(raw, 0.0) + jnp.log1p(jnp.exp(-jnp.abs(raw)))
        cum = exact_times(lower, dt * rate)
        last = cum[STRETCH - 1 :, :]
        r.raw[q] = raw
        r.dt[q] = dt
        weight = jnp.exp(last - cum) * dt
        growth = jnp.exp(cum)
        r.tot_send[pl.ds(q, 1), :] = last
        r.tot_send[pl.ds(seqs + q, 1), :] = X_B * jnp.sum(weight, axis=0, keepdims=True)
        r.tot_send[pl.ds(2 * seqs + q, 1), :] = GY_C * jnp.sum(growth, axis=0, keepdims=True)
        r.weight[q] = weight
        r.cum[q] = cum
        r.e_wide[q] = times_exact(growth, spread)

    def send_tot(k):
        remote(r.tot_send, r.tot_all.at[s], TOT, (seq_peer(k), h))

    over(ns - 1, send_tot)
    r.tot_all[s] = r.tot_send[...]
    r.own_wide[...] = times_exact(r.tot_send[...], spread)

    def own_bound(row):
        return r.own_wide[pl.ds(row, 1), :]

    own[0].wait()
    arrived(r.c_all.at[:, 0 : chips - 1, 0], C)
    remote(r.c_all.at[:, :, core], r.c_all.at[:, :, core], C2, other)
    for q in range(seqs):
        first, second = split(r.gy[q].astype(F32) * r.e_wide[q], 2)
        r.gys_hi[q] = first
        r.gys_lo[q] = second
    arrived(r.c_all.at[:, :, 0], C2)

    def c_of(q):
        return r.c_all[q].reshape(STRETCH, STATE)

    def b_of(q):
        return r.b_all[q].reshape(STRETCH, STATE)

    def x_of(q):
        return r.x_all[q].reshape(STRETCH, width)

    def piece(c):
        return pl.ds(c * half, half)

    def send_parts(q, source, target, sem, cols):
        def one(k):
            peer = seq_peer(k)
            remote(source.at[q, columns(peer, part), cols], target.at[q, s, :, cols], sem, (peer, h))

        over(ns - 1, one)
        target[q, s, :, cols] = source[q, columns(s, part), cols]

    for q in range(seqs):
        for c in range(CUTS):
            cols = piece(c)
            state = dot(c_of(q), r.gys_hi[q, :, cols], TN) + dot(c_of(q), r.gys_lo[q, :, cols], TN)
            r.g_out[q, :, cols] = encode(state, r.own_wide[pl.ds(2 * seqs + q, 1), cols])
            send_parts(q, r.g_out, r.g_in, G + q * CUTS + c, cols)

    for q in range(seqs):
        cum = r.cum[q]
        r.w_wide[q] = times_exact(r.weight[q], spread)
        r.u_row[q] = jnp.transpose(cum - jnp.log(r.dt[q]))[:heads, :]
        for e in range(heads):
            r.cum_col[q, e] = jnp.broadcast_to(cum[:, e : e + 1], (STRETCH, LANES))

    own[1].wait()
    arrived(r.b_all.at[:, 0 : chips - 1, 0], B)
    remote(r.b_all.at[:, :, core], r.b_all.at[:, :, core], B2, other)
    arrived(r.b_all.at[:, :, 0], B2)

    def decays(q, c):
        if c == 0:
            r.scores[q] = dot(c_of(q), b_of(q), NT)

        def one(i):
            e = c * (heads // CUTS) + i
            column = r.cum_col[q, e]
            gap = jnp.concatenate([column, column], axis=1) - r.u_row[q, pl.ds(e, 1), :]
            decay = jnp.where(causal, jnp.exp(gap), 0.0)
            r.decay[q, e] = decay
            first, second = split(r.scores[q] * decay, 2)
            r.mix_hi[q, e] = first
            r.mix_lo[q, e] = second
            rows_e = columns(e, HEAD_DIM)
            grad = r.gy_t[q, rows_e, :]
            r.z_t[q, rows_e, :] = dot(grad, first) + dot(grad, second)

        over(heads // CUTS, one)

    def send_state(q):
        arrived(r.x_all.at[q, 0 : nh - 1], X + q)
        first, second = split(x_of(q).astype(F32) * r.w_wide[q], 2)
        r.xs_hi[q] = first
        r.xs_lo[q] = second
        state = dot(b_of(q), first, TN) + dot(b_of(q), second, TN)
        r.f_out[q] = encode(state, own_bound(seqs + q))
        send_parts(q, r.f_out, r.f_in, F + q, pl.ds(0, width))

    def within(q):
        r.d_scores[q] = jnp.zeros((STRETCH, STRETCH), F32)
        low = iota((STRETCH, LANES), 1) < HEAD_DIM

        def one(i):
            cols = columns(i, LANES)
            x_pair = r.x_all[q, :, :, cols].reshape(STRETCH, LANES)
            grad = r.gy[q, :, cols].astype(F32)
            results = []
            total = r.d_scores[q]
            for k in range(2):
                e = 2 * i + k
                results.append(dot(r.mix_hi[q, e], x_pair) + dot(r.mix_lo[q, e], x_pair))
                masked = jnp.where(low if k == 0 else ~low, grad, 0.0).astype(BF16)
                total = total + dot(masked, x_pair, NT) * r.decay[q, e]
            r.d_scores[q] = total
            r.y_in[q, :, cols] = jnp.where(low, results[0], results[1])

        over(heads // 2, one)

    def scan(q, source, result, bounds, target, sem, sem_in, bound_row, reverse, cols):
        arrived(source.at[q, 0 : ns - 1, :, cols], sem_in)

        def wide(block, row):
            return r.wide[pl.ds(block * 8 + row, 1), cols]

        def one(i, carry):
            block = ns - 1 - i if reverse else i
            state, bound = carry
            bounds[q, block, :, cols] = bound
            result[q, block, :, cols] = encode(state, bound)
            factor = jnp.exp(wide(block, q))
            block_bound = wide(block, bound_row + q)
            return (
                factor * state + decode(source[q, block, :, cols], block_bound),
                factor * bound + block_bound,
            )

        start = (jnp.zeros((part, cols.size), F32), jnp.zeros((1, cols.size), F32))
        lax.fori_loop(0, ns, one, start, unroll=8)

        def back(k):
            peer = seq_peer(k)
            remote(
                result.at[q, peer, :, cols], target.at[q, columns(s, part), cols], sem, (peer, h)
            )

        over(ns - 1, back)
        target[q, columns(s, part), cols] = result[q, s, :, cols]

    def scan_back(q, c):
        number = q * CUTS + c
        scan(q, r.g_in, r.g_res, r.d_bound, r.d_code, D + number, G + number, 2 * seqs, True, piece(c))

    def scan_on(q):
        scan(q, r.f_in, r.f_res, r.s_bound, r.s_code, S + q, F + q, seqs, False, pl.ds(0, width))

    def states_here(q, codes, bounds, target, sem, cols):
        arrived(codes.at[q, 0 : (ns - 1) * part, cols], sem)
        target[q, :, cols] = decode(codes[q, :, cols], bounds[q, s, :, cols])

    own_gx = []

    def grad_x(q, c):
        cols = piece(c)
        states_here(q, r.d_code, r.d_bound, r.d_all, D + q * CUTS + c, cols)
        xc = r.w_wide[q, :, cols] * dot_split(b_of(q), r.d_all[q, :, cols])
        xp = jnp.transpose(r.z_t[q, cols, :]) + xc
        r.xc[q, :, cols] = xc
        r.xp[q, :, cols] = xp
        skip = skip_row[:, c * half : (c + 1) * half]
        r.gx[q, :, cols] = (skip * r.gy[q, :, cols].astype(F32) + xp).astype(BF16)
        slot = r.gx_out.at[q, :, columns(h * CUTS + c, half)]

        def one(k):
            peer = head_peer(k)
            remote(r.gx.at[q, columns(peer, rows), cols], slot, GX + q, (s, peer))

        over(nh - 1, one)
        own_gx.append(local(r.gx.at[q, columns(h, rows), cols], slot, 4 + q * CUTS + c))

    def hand_over(q, value, slices, sem):
        slices[q] = value.astype(BF16).reshape(chips, 2, rows, STATE)
        remote(slices.at[q, :, 1 - core], slices.at[seqs + q, :, 0], sem + q, other)

    own_group = []

    def join(q, slices, sums, out, sem_in, sem, number):
        arrived(slices.at[seqs + q, :, 0], sem_in + q)
        sums[q] = (slices[q, :, core].astype(F32) + slices[seqs + q, :, 0].astype(F32)).astype(BF16)

        def slot():
            return out.at[q, :, columns(chip, STATE)]

        def one(k):
            peer = same_core_peer(k)
            remote(sums.at[q, peer // 2], slot(), sem + q, (s, peer))

        over(chips - 1, one)
        own_group.append(local(sums.at[q, chip], slot(), number))

    def grad_b(q):
        first, second = split(jnp.transpose(r.d_scores[q]), 2)
        value = dot(first, c_of(q)) + dot(second, c_of(q))
        d_hi, d_lo = split(r.d_all[q], 2)
        value = value + dot(r.xs_hi[q], d_hi, NT)
        value = value + (dot(r.xs_hi[q], d_lo, NT) + dot(r.xs_lo[q], d_hi, NT))
        hand_over(q, value, r.gb, GB2)

    def join_b(q):
        join(q, r.gb, r.gb_sum, r.gb_out, GB2, GB, 4 + CUTS * seqs + q)

    def join_c(q):
        join(q, r.gc, r.gc_sum, r.gc_out, GC2, GC, 4 + (CUTS + 1) * seqs + q)

    def grad_c(q):
        states_here(q, r.s_code, r.s_bound, r.s_all, S + q, pl.ds(0, width))
        s_hi, s_lo = split(r.s_all[q], 2)
        value = r.gc_in[q] + dot(r.gys_hi[q], s_hi, NT)
        value = value + (dot(r.gys_hi[q], s_lo, NT) + dot(r.gys_lo[q], s_hi, NT))
        hand_over(q, value, r.gc, GC2)

    def before_state(q):
        x = x_of(q).astype(F32)
        r.v[q] = times_exact(x * r.xp[q], gather)
        r.at_last[q] = jnp.sum(x * r.xc[q], axis=0, keepdims=True)
        first, second = split(r.d_scores[q], 2)
        r.gc_in[q] = dot(first, b_of(q)) + dot(second, b_of(q))

    def outputs(q):
        y = r.y_in[q] + r.e_wide[q] * dot_split(c_of(q), r.s_all[q])
        dt = r.dt[q]
        v = r.v[q]
        d_cum = times_exact(r.gy[q].astype(F32) * y, gather) - v
        at_last = r.at_last[q] + r.e_wide[q, STRETCH - 1 :, :] * jnp.sum(
            r.s_all[q] * r.d_all[q], axis=0, keepdims=True
        )
        at_last = times_exact(jnp.broadcast_to(at_last, (8, width)), gather)[:1]
        d_sum = exact_times(upper, d_cum) + at_last
        r.gd_wide[q] = (v / dt + rate * d_sum) * jax.nn.sigmoid(r.raw[q])
        r.y_out[q] = (y + skip_row * x_of(q).astype(F32)).astype(BF16)

    def send_steps():
        for q in range(seqs):
            values = dot(r.gd_wide[q].astype(BF16), one_hot(lane_of_head))
            values = jnp.where(token_lane, values, 0.0).reshape(nh, rows, LANES).sum(axis=1)
            for p in range(nh):
                r.gd_pack[p, :, q * LANES : (q + 1) * LANES] = values[p : p + 1, :]

        def one(k):
            peer = head_peer(k)
            remote(r.gd_pack.at[peer], r.gd_all.at[h], GD, (s, peer))

        over(nh - 1, one)
        r.gd_all[h] = r.gd_pack[h]

    decays(0, 0)
    arrived(r.tot_all.at[0 : ns - 1], TOT)
    r.wide[...] = times_exact(r.tot_all[...].reshape(ns * 8, LANES), spread)
    scan_back(0, 0)
    own[2].wait()
    send_state(0)
    decays(1, 0)
    scan_back(1, 0)
    within(0)
    send_state(1)
    grad_x(0, 0)
    scan_on(0)
    within(1)
    before_state(0)
    grad_b(0)
    grad_x(1, 0)
    scan_on(1)
    grad_b(1)
    before_state(1)
    join_b(0)
    grad_c(0)
    join_b(1)
    outputs(0)
    join_c(0)
    grad_c(1)
    outputs(1)
    send_steps()
    join_c(1)

    arrived(r.gd_all.at[0 : nh - 1], GD)
    for q in range(seqs):
        r.gdt_out[q] = regrouped(lambda i, q=q: r.gd_all[i, :, q * LANES : (q + 1) * LANES]).astype(BF16)
    for q in range(seqs):
        arrived(r.gx_out.at[q, :, 0 : (nh - 1) * width], GX + q)
        arrived(r.gb_out.at[q, :, 0 : (chips - 1) * STATE], GB + q)
        arrived(r.gc_out.at[q, :, 0 : (chips - 1) * STATE], GC + q)

    left(r.dt_all.at[0 : nh - 1], DT)
    left(r.gd_all.at[0 : nh - 1], GD)
    left(r.c_all.at[:, 0 : chips - 1, 0], C)
    left(r.c_all.at[:, :, 0], C2)
    left(r.b_all.at[:, 0 : chips - 1, 0], B)
    left(r.b_all.at[:, :, 0], B2)
    left(r.tot_all.at[0 : ns - 1], TOT)
    for q in range(seqs):
        left(r.x_all.at[q, 0 : nh - 1], X + q)
        for c in range(CUTS):
            left(r.g_in.at[q, 0 : ns - 1, :, piece(c)], G + q * CUTS + c)
            left(r.g_res.at[q, 0 : ns - 1, :, piece(c)], D + q * CUTS + c)
        left(r.f_in.at[q, 0 : ns - 1], F + q)
        left(r.f_res.at[q, 0 : ns - 1], S + q)
        left(r.gx.at[q, 0 : (nh - 1) * rows, :], GX + q)
        left(r.gb.at[q, :, 0], GB2 + q)
        left(r.gc.at[q, :, 0], GC2 + q)
        left(r.gb_sum.at[q, 0 : chips - 1], GB + q)
        left(r.gc_sum.at[q, 0 : chips - 1], GC + q)
    for copy in own_gx + own_group:
        copy.wait()


def deliver(*refs):
    count = len(refs) // 2
    copies = [pltpu.make_async_copy(refs[i], refs[count + i], refs[-1].at[i]) for i in range(count)]
    for copy in copies:
        copy.start()
    for copy in copies:
        copy.wait()


def on_device(x_in, b_in, c_in, dt_in, a_log, skip_gain, grad_y):
    ns, nh = lax.axis_size("seq"), lax.axis_size("head")
    seqs, rows, all_heads = dt_in.shape
    heads = a_log.shape[0]
    width = heads * HEAD_DIM
    part = STATE // ns
    chips = nh // 2
    scratch = {
        "regroup": ((nh * LANES, LANES), BF16),
        "dt_pack": ((nh, 1, seqs * LANES), F32),
        "dt_all": ((nh, 1, seqs * LANES), F32),
        "c_all": ((seqs, chips, 2, rows, STATE), BF16),
        "b_all": ((seqs, chips, 2, rows, STATE), BF16),
        "x_all": ((seqs, nh, rows, width), BF16),
        "gy": ((seqs, STRETCH, width), BF16),
        "gy_t": ((seqs, width, STRETCH), BF16),
        "raw": ((seqs, STRETCH, LANES), F32),
        "dt": ((seqs, STRETCH, LANES), F32),
        "weight": ((seqs, STRETCH, LANES), F32),
        "cum": ((seqs, STRETCH, LANES), F32),
        "tot_send": ((8, LANES), F32),
        "tot_all": ((ns, 8, LANES), F32),
        "wide": ((ns * 8, width), F32),
        "own_wide": ((8, width), F32),
        "w_wide": ((seqs, STRETCH, width), F32),
        "e_wide": ((seqs, STRETCH, width), F32),
        "u_row": ((seqs, heads, STRETCH), F32),
        "cum_col": ((seqs, heads, STRETCH, LANES), F32),
        "gys_hi": ((seqs, STRETCH, width), BF16),
        "gys_lo": ((seqs, STRETCH, width), BF16),
        "xs_hi": ((seqs, STRETCH, width), BF16),
        "xs_lo": ((seqs, STRETCH, width), BF16),
        "scores": ((seqs, STRETCH, STRETCH), F32),
        "d_scores": ((seqs, STRETCH, STRETCH), F32),
        "decay": ((seqs, heads, STRETCH, STRETCH), F32),
        "mix_hi": ((seqs, heads, STRETCH, STRETCH), BF16),
        "mix_lo": ((seqs, heads, STRETCH, STRETCH), BF16),
        "z_t": ((seqs, width, STRETCH), F32),
        "v": ((seqs, STRETCH, LANES), F32),
        "at_last": ((seqs, 1, width), F32),
        "gc_in": ((seqs, STRETCH, STATE), F32),
        "xc": ((seqs, STRETCH, width), F32),
        "xp": ((seqs, STRETCH, width), F32),
        "y_in": ((seqs, STRETCH, width), F32),
        "gx": ((seqs, STRETCH, width), BF16),
        "gb": ((2 * seqs, chips, 2, rows, STATE), BF16),
        "gc": ((2 * seqs, chips, 2, rows, STATE), BF16),
        "gb_sum": ((seqs, chips, rows, STATE), BF16),
        "gc_sum": ((seqs, chips, rows, STATE), BF16),
        "gd_wide": ((seqs, STRETCH, LANES), F32),
        "gd_pack": ((nh, 1, seqs * LANES), F32),
        "gd_all": ((nh, 1, seqs * LANES), F32),
    }
    for name in ("g", "f"):
        scratch[name + "_out"] = ((seqs, STATE, width), BF16)
        scratch[name + "_in"] = ((seqs, ns, part, width), BF16)
        scratch[name + "_res"] = ((seqs, ns, part, width), BF16)
    for name in ("d", "s"):
        scratch[name + "_all"] = ((seqs, STATE, width), F32)
        scratch[name + "_code"] = ((seqs, STATE, width), BF16)
        scratch[name + "_bound"] = ((seqs, ns, 1, width), F32)
    sems = 7 + (8 + 2 * CUTS) * seqs
    names = (
        ["a_log", "skip", "x_in", "b_in", "c_in", "dt_in", "gy_in"]
        + ["y_out", "gx_out", "gb_out", "gc_out", "gdt_out"]
        + list(scratch)
        + ["send_sem", "recv_sem", "local_sem"]
    )
    dims = (ns, nh, seqs, rows, heads)

    def body(*refs):
        mixer(dims, names, *refs)

    anywhere = pl.BlockSpec(memory_space=pl.ANY)
    small = pl.BlockSpec(memory_space=pltpu.SMEM)
    vmem = pl.BlockSpec(memory_space=pltpu.VMEM)

    def like(array):
        return jax.ShapeDtypeStruct(array.shape, BF16)

    results = pl.pallas_call(
        body,
        out_shape=tuple(pltpu.VMEM(array.shape, BF16) for array in (grad_y, x_in, b_in, c_in, dt_in)),
        in_specs=[small, small, anywhere, anywhere, anywhere, vmem, anywhere],
        out_specs=(vmem,) * 5,
        scratch_shapes=[pltpu.VMEM(shape, dtype) for shape, dtype in scratch.values()]
        + [
            pltpu.SemaphoreType.DMA((sems,)),
            pltpu.SemaphoreType.DMA((sems,)),
            pltpu.SemaphoreType.DMA((4 + (CUTS + 2) * seqs,)),
        ],
        compiler_params=pltpu.CompilerParams(
            collective_id=0, has_side_effects=True, vmem_limit_bytes=56 * 1024 * 1024
        ),
        name="mixer",
    )(a_log, skip_gain, x_in, b_in, c_in, dt_in, grad_y)
    results = [pltpu.with_memory_space_constraint(result, pltpu.VMEM) for result in results]
    return pl.pallas_call(
        deliver,
        out_shape=tuple(like(result) for result in results),
        in_specs=[anywhere] * len(results),
        out_specs=(anywhere,) * len(results),
        scratch_shapes=[pltpu.SemaphoreType.DMA((len(results),))],
        name="deliver",
    )(*results)


def solution(mesh):
    spread = P(None, ("seq", "head"), None)
    return jax.shard_map(
        on_device,
        mesh=mesh,
        in_specs=(spread, spread, spread, spread, P("head"), P("head"), P(None, "seq", "head")),
        out_specs=(P(None, "seq", "head"), spread, spread, spread, spread),
        check_vma=False,
    )
```
